256 devices in a mesh: lat: 8 (over y_hi, x), lon: 32 (over y_lo, z, core).
Axes of the slice: x: 4, y: 4 (y_hi: 2, y_lo: 2; y = y_hi * 2 + y_lo), z: 8, core: 2. Of those that a mesh axis runs over, the one named last changes fastest.
Arguments:
- queries: bfloat16 [64, 512, 1024], P('lat', 'lon'), may hold values from -180 to 180
- keys: bfloat16 [64, 512, 1024], P('lat', 'lon'), may hold values from -6 to 6
- values: bfloat16 [64, 512, 1024], P('lat', 'lon'), may hold values from -6 to 6
- cotangent: bfloat16 [64, 512, 1024], P('lat', 'lon'), may hold values from -6 to 6
- near_pattern: int32 [16, 13, 13], replicated, may hold values 0 or 1
- zonal_pattern: int32 [64, 32], P('lat'), may hold values 0 or 1
Outputs:
- attended: bfloat16 [64, 512, 1024], P('lat', 'lon')
- grad_queries: bfloat16 [64, 512, 1024], P('lat', 'lon')
- grad_keys: bfloat16 [64, 512, 1024], P('lat', 'lon')
- grad_values: bfloat16 [64, 512, 1024], P('lat', 'lon')
The draws below stay inside these ranges and needn't reach their ends.
All inputs are finite; a program needn't handle non-finite values. No bound on the sum of `zonal_pattern` on one device may be relied on, other than what follows from the above.
Results may differ from the reference program's by a relative error of at most 0.014.
Values may be sent and summed in bfloat16 or wider, within the bound.
A program may use at most 128 MiB of HBM per device.

```python
import jax
import jax.numpy as jnp
import numpy as np
from jax import lax

D = 1024
HEADS = 16
HEAD_DIM = 64
RADIUS = 6
LS = 16
SECT = 32
LAT = 64
LON = 512


def shared_normal(key):
    return jnp.clip(jax.random.normal(key, (LAT, LON, D), jnp.float32), -6.0, 6.0)


def draw_keys(key, part):
    base = shared_normal(key)
    return base.astype(jnp.bfloat16)


def draw_queries(key, part):
    key = jax.random.fold_in(key, 7)
    first_key = jax.random.fold_in(key, 0)
    fresh = jnp.clip(jax.random.normal(first_key, (LAT, LON, D), jnp.float32), -6.0, 6.0)
    return fresh.astype(jnp.bfloat16)


def plant(drawn, key, least, largest):
    spot = [jax.random.randint(jax.random.fold_in(key, axis), (), 0, length) for axis, length in enumerate(drawn.shape)]
    widest = drawn.shape.index(max(drawn.shape))
    next_to = spot[:widest] + [(spot[widest] + 1) % drawn.shape[widest]] + spot[widest + 1:]
    return drawn.at[tuple(spot)].set(least).at[tuple(next_to)].set(largest)


def levels(own_key, shape, pieces, smallest, high):
    def one(axis_at, blocks):
        draws = jax.random.uniform(jax.random.fold_in(jax.random.fold_in(own_key, 6), axis_at), (blocks,), jnp.float32, smallest / len(pieces), high / len(pieces))
        return jnp.repeat(jnp.exp(draws), shape[axis_at] // blocks).reshape((-1,) + (1,) * (len(shape) - axis_at - 1))

    level = one(*pieces[0])
    for cut in pieces[1:]:
        level = level * one(*cut)
    return level


def normal_values(key, extent, spread, bound, cuts=(), kind=jnp.bfloat16):
    values = jax.random.normal(key, extent, jnp.float32) * spread
    if len(cuts) > 0:
        values = levels(key, extent, cuts, -0.22, 0.18) * values
    return jnp.clip(values, min=-bound, max=bound).astype(kind)


def setup_inputs(seed: int = 0) -> dict:
    seeds = jax.random.split(jax.random.key(seed), 7)
    queries = draw_queries(jax.random.fold_in(seeds[6], 71), 0)
    keys = draw_keys(jax.random.fold_in(seeds[6], 71), 0)
    values = normal_values(seeds[2], (LAT, LON, D), 1.0, 6.0, ((0, 8), (1, 32)))
    cotangent = normal_values(seeds[3], (LAT, LON, D), 1.0, 6.0, ((0, 8), (1, 32)))
    near_pattern = plant((jax.random.randint(seeds[4], (HEADS, 2 * RADIUS + 1, 2 * RADIUS + 1), 0, 4) < 3).astype(jnp.int32), jax.random.fold_in(seeds[4], 1), 0, 1)
    zonal_pattern = plant((jax.random.randint(seeds[5], (LAT, SECT), 0, 2) < 1).astype(jnp.int32), jax.random.fold_in(seeds[5], 1), 0, 1)
    return dict(queries=queries, keys=keys, values=values, cotangent=cotangent, near_pattern=near_pattern, zonal_pattern=zonal_pattern)


def rounded(values_in):
    return lax.optimization_barrier(values_in.astype(jnp.bfloat16)).astype(jnp.float32)


def offset_tables(tile_rows, tile_cols):
    window_span = 2 * RADIUS + 1
    region_rows = tile_rows + 2 * RADIUS
    region_cols = tile_cols + 2 * RADIUS
    query_rows = np.repeat(np.arange(tile_rows), tile_cols)
    query_cols = np.tile(np.arange(tile_cols), tile_rows)
    key_rows = np.repeat(np.arange(region_rows), region_cols)
    key_cols = np.tile(np.arange(region_cols), region_rows)
    down_offset = key_rows[None, :] - query_rows[:, None]
    side_offset = key_cols[None, :] - query_cols[:, None]
    in_window = (down_offset >= 0) & (down_offset < window_span) & (side_offset >= 0) & (side_offset < window_span)
    offset_index = np.where(in_window, down_offset * window_span + side_offset, 0)
    return offset_index, in_window, key_rows


def near_allowed(near_pattern):
    window_span = 2 * RADIUS + 1
    pattern_flat = near_pattern.reshape(near_pattern.shape[0], window_span * window_span) == 1
    centre = jnp.arange(window_span * window_span) == RADIUS * window_span + RADIUS
    return pattern_flat | centre[None, :]


def wrap_pad(grid):
    widened = jnp.concatenate([grid[:, LON - RADIUS:], grid, grid[:, :RADIUS]], axis=1)
    return jnp.pad(widened, ((RADIUS, RADIUS), (0, 0), (0, 0)))


def pool_rows(grid):
    return jnp.sum(grid.astype(jnp.float32).reshape(LAT, SECT, LS, D), axis=2) * LS ** -0.5


def reference(queries, keys, values, cotangent, near_pattern, zonal_pattern):
    softmax_scale = HEAD_DIM ** -0.5
    tile_rows = 8
    tile_cols = min(LS, 32)
    region_rows = tile_rows + 2 * RADIUS
    region_cols = tile_cols + 2 * RADIUS
    count_q = tile_rows * tile_cols
    count_k = region_rows * region_cols
    lat_tiles = LAT // tile_rows
    lon_tiles = LON // tile_cols
    tile_total = lat_tiles * lon_tiles
    offset_index, in_window, key_rows = offset_tables(tile_rows, tile_cols)
    base_mask = near_allowed(near_pattern)[:, offset_index] & in_window[None]
    row_valid = jnp.pad(jnp.ones((LAT,), bool), RADIUS)
    pooled_keys = rounded(pool_rows(keys))
    pooled_values = rounded(pool_rows(values))
    zonal_ok = zonal_pattern == 1
    key_pad = wrap_pad(keys).astype(jnp.float32)
    value_pad = wrap_pad(values).astype(jnp.float32)
    query_full = queries.astype(jnp.float32)
    grad_full = cotangent.astype(jnp.float32)
    highest = lax.Precision.HIGHEST
    zero_index = jnp.int32(0)

    def tile_inputs(tile_number):
        row_start = ((tile_number // lon_tiles) * tile_rows).astype(jnp.int32)
        col_start = ((tile_number % lon_tiles) * tile_cols).astype(jnp.int32)
        query_tile = lax.dynamic_slice(query_full, (row_start, col_start, zero_index), (tile_rows, tile_cols, D))
        grad_tile = lax.dynamic_slice(grad_full, (row_start, col_start, zero_index), (tile_rows, tile_cols, D))
        key_block = lax.dynamic_slice(key_pad, (row_start, col_start, zero_index), (region_rows, region_cols, D))
        value_block = lax.dynamic_slice(value_pad, (row_start, col_start, zero_index), (region_rows, region_cols, D))
        sector_keys = lax.dynamic_slice(pooled_keys, (row_start, zero_index, zero_index), (tile_rows, SECT, D))
        sector_values = lax.dynamic_slice(pooled_values, (row_start, zero_index, zero_index), (tile_rows, SECT, D))
        sector_ok = lax.dynamic_slice(zonal_ok, (row_start, zero_index), (tile_rows, SECT))
        rows_ok = lax.dynamic_slice(row_valid, (row_start,), (region_rows,))
        admitted = base_mask & rows_ok[key_rows][None, None, :]
        zonal_mask = jnp.broadcast_to(sector_ok[:, None, :], (tile_rows, tile_cols, SECT)).reshape(count_q, SECT)[None]
        return row_start, col_start, query_tile, grad_tile, key_block, value_block, sector_keys, sector_values, admitted, zonal_mask

    def tile_scores(query_tile, key_block, sector_keys):
        near_score = jnp.einsum('qhd,khd->hqk', query_tile.reshape(count_q, HEADS, HEAD_DIM), key_block.reshape(count_k, HEADS, HEAD_DIM), precision=highest) * softmax_scale
        zonal_score = jnp.einsum('rchd,rshd->hrcs', query_tile.reshape(tile_rows, tile_cols, HEADS, HEAD_DIM), sector_keys.reshape(tile_rows, SECT, HEADS, HEAD_DIM), precision=highest).reshape(HEADS, count_q, SECT) * softmax_scale
        return near_score, zonal_score

    def forward_tile(tile_number):
        row_start, col_start, query_tile, grad_tile, key_block, value_block, sector_keys, sector_values, admitted, zonal_mask = tile_inputs(tile_number)
        near_score, zonal_score = tile_scores(query_tile, key_block, sector_keys)
        highest_score = jnp.maximum(jnp.max(jnp.where(admitted, near_score, -jnp.inf), axis=2), jnp.max(jnp.where(zonal_mask, zonal_score, -jnp.inf), axis=2))
        denominator = jnp.sum(jnp.where(admitted, jnp.exp(near_score - highest_score[..., None]), 0.0), axis=2) + jnp.sum(jnp.where(zonal_mask, jnp.exp(zonal_score - highest_score[..., None]), 0.0), axis=2)
        tile_lse = highest_score + jnp.log(denominator)
        near_weights = rounded(jnp.where(admitted, jnp.exp(near_score - tile_lse[..., None]), 0.0))
        zonal_weights = jnp.where(zonal_mask, jnp.exp(zonal_score - tile_lse[..., None]), 0.0)
        tile_output = jnp.einsum('hqk,khd->qhd', near_weights, value_block.reshape(count_k, HEADS, HEAD_DIM), precision=highest)
        tile_output = tile_output + jnp.einsum('hrcs,rshd->rchd', zonal_weights.reshape(HEADS, tile_rows, tile_cols, SECT), sector_values.reshape(tile_rows, SECT, HEADS, HEAD_DIM), precision=highest).reshape(count_q, HEADS, HEAD_DIM)
        return tile_output.reshape(count_q, D), tile_lse

    def to_grid(tiled):
        return tiled.reshape(lat_tiles, lon_tiles, tile_rows, tile_cols, D).transpose(0, 2, 1, 3, 4).reshape(LAT, LON, D)

    tile_outputs, tile_lses = lax.map(forward_tile, jnp.arange(tile_total, dtype=jnp.int32))
    unrounded = to_grid(tile_outputs)
    attended = unrounded.astype(jnp.bfloat16)
    deltas = jnp.sum(grad_full.reshape(LAT, LON, HEADS, HEAD_DIM) * unrounded.reshape(LAT, LON, HEADS, HEAD_DIM), axis=3)

    def backward_tile(state, tile_number):
        grad_pad, pooled_grads = state
        row_start, col_start, query_tile, grad_tile, key_block, value_block, sector_keys, sector_values, admitted, zonal_mask = tile_inputs(tile_number)
        near_score, zonal_score = tile_scores(query_tile, key_block, sector_keys)
        tile_lse = tile_lses[tile_number]
        tile_deltas = lax.dynamic_slice(deltas, (row_start, col_start, zero_index), (tile_rows, tile_cols, HEADS)).reshape(count_q, HEADS).T
        query_heads = query_tile.reshape(count_q, HEADS, HEAD_DIM)
        grad_heads = grad_tile.reshape(count_q, HEADS, HEAD_DIM)
        key_heads = key_block.reshape(count_k, HEADS, HEAD_DIM)
        value_heads = value_block.reshape(count_k, HEADS, HEAD_DIM)
        near_prob = jnp.where(admitted, jnp.exp(near_score - tile_lse[..., None]), 0.0)
        near_weights = rounded(near_prob)
        near_dot = jnp.einsum('qhd,khd->hqk', grad_heads, value_heads, precision=highest)
        near_grads = rounded(near_prob * (near_dot - tile_deltas[..., None]) * softmax_scale)
        zonal_prob = jnp.where(zonal_mask, jnp.exp(zonal_score - tile_lse[..., None]), 0.0)
        grid_grads = grad_tile.reshape(tile_rows, tile_cols, HEADS, HEAD_DIM)
        grid_queries = query_tile.reshape(tile_rows, tile_cols, HEADS, HEAD_DIM)
        sector_key_heads = sector_keys.reshape(tile_rows, SECT, HEADS, HEAD_DIM)
        sector_value_heads = sector_values.reshape(tile_rows, SECT, HEADS, HEAD_DIM)
        zonal_dot = jnp.einsum('rchd,rshd->hrcs', grid_grads, sector_value_heads, precision=highest).reshape(HEADS, count_q, SECT)
        zonal_grads = rounded(zonal_prob * (zonal_dot - tile_deltas[..., None]) * softmax_scale).reshape(HEADS, tile_rows, tile_cols, SECT)
        zonal_probs = rounded(zonal_prob).reshape(HEADS, tile_rows, tile_cols, SECT)
        query_grad = jnp.einsum('hqk,khd->qhd', near_grads, key_heads, precision=highest)
        query_grad = query_grad + jnp.einsum('hrcs,rshd->rchd', zonal_grads, sector_key_heads, precision=highest).reshape(count_q, HEADS, HEAD_DIM)
        key_grad = jnp.einsum('hqk,qhd->khd', near_grads, query_heads, precision=highest)
        value_grad = jnp.einsum('hqk,qhd->khd', near_weights, grad_heads, precision=highest)
        section = jnp.stack([key_grad, value_grad]).reshape(2, region_rows, region_cols, D)
        corner = (zero_index, row_start, col_start, zero_index)
        grad_pad = lax.dynamic_update_slice(grad_pad, lax.dynamic_slice(grad_pad, corner, (2, region_rows, region_cols, D)) + section, corner)
        pooled_key_grad = jnp.einsum('hrcs,rchd->rshd', zonal_grads, grid_queries, precision=highest)
        pooled_value_grad = jnp.einsum('hrcs,rchd->rshd', zonal_probs, grid_grads, precision=highest)
        pooled_section = jnp.stack([pooled_key_grad, pooled_value_grad]).reshape(2, tile_rows, SECT, D)
        sector_corner = (zero_index, row_start, zero_index, zero_index)
        pooled_grads = lax.dynamic_update_slice(pooled_grads, lax.dynamic_slice(pooled_grads, sector_corner, (2, tile_rows, SECT, D)) + pooled_section, sector_corner)
        return (grad_pad, pooled_grads), query_grad.reshape(count_q, D)

    initial = (jnp.zeros((2, LAT + 2 * RADIUS, LON + 2 * RADIUS, D), jnp.float32), jnp.zeros((2, LAT, SECT, D), jnp.float32))
    (grad_pad, pooled_grads), query_grads = lax.scan(backward_tile, initial, jnp.arange(tile_total, dtype=jnp.int32))
    banded = grad_pad[:, RADIUS:LAT + RADIUS]
    interior = banded[:, :, RADIUS:LON + RADIUS]
    interior = interior.at[:, :, LON - RADIUS:].add(banded[:, :, :RADIUS])
    interior = interior.at[:, :, :RADIUS].add(banded[:, :, LON + RADIUS:])
    interior = interior + jnp.repeat(pooled_grads, LS, axis=2) * LS ** -0.5
    grad_queries = to_grid(query_grads).astype(jnp.bfloat16)
    return attended, grad_queries, interior[0].astype(jnp.bfloat16), interior[1].astype(jnp.bfloat16)
```

```python
import jax
import jax.numpy as jnp
from jax import lax
from jax.experimental import pallas as pl
from jax.experimental.pallas import tpu as pltpu
from jax.sharding import PartitionSpec as P

MESH = pl.DeviceIdType.MESH
RADIUS = 6
SPAN = 2 * RADIUS + 1
ROWS = 8
COLS = 16
REGION = ROWS + 2 * RADIUS
SECT = 32
ZN = 8
LANES = 256
CHUNKS = 4
TILES = 56
CENTRE, LEFT, RIGHT, ZONAL = 0, 20, 30, 40
NEVER = -1e30
BF, F32 = jnp.bfloat16, jnp.float32


def kernel(
    q_ref, k_ref, v_ref, do_ref, near_ref, zonal_ref,
    att_ref, gq_ref, gk_ref, gv_ref,
    kv, edge, corner, gath, bias, bias_z, wide, scores, probs,
    acc, side_out, side_in, lat_out, lat_in,
    z_out, z_in1, z_mid1, z_in2, z_mid2, z_in3,
    lat_s, lat_r, edge_s, edge_r, cor_s, cor_r,
    g_s, g_r, gy_s, gy_r, gc_s, gc_r, gd_s, gd_r,
    side_s, side_r, glat_s, glat_r, zc_s, zc_r, zy_s, zy_r, zz_s, zz_r,
):
    lat, lon = lax.axis_index("lat"), lax.axis_index("lon")
    lats, lons = lax.axis_size("lat"), lax.axis_size("lon")
    core, zed, why = lon % 2, (lon // 2) % ZN, lon // (2 * ZN)

    def lon_of(y, z, c):
        return (y * ZN + z) * 2 + c

    up, down = (lat + lats - 1) % lats, (lat + 1) % lats
    west, east = (lon + lons - 1) % lons, (lon + 1) % lons
    core_peer = lon_of(why, zed, 1 - core)
    y_peer = lon_of(1 - why, zed, core)
    z_peers = [None] + [lon_of(why, (zed + d) % ZN, core) for d in range(1, ZN)]
    z_from = [lon_of(why, (zed + ZN - d) % ZN, core) for d in range(ZN)]

    barrier = pltpu.get_barrier_semaphore()
    greeted = [(up, lon), (down, lon), (lat, west), (lat, east), (lat, core_peer), (lat, y_peer)]
    greeted += [(lat, peer) for peer in z_peers[1:]]
    for peer in greeted:
        pl.semaphore_signal(barrier, inc=1, device_id=peer, device_id_type=MESH)

    def remote(src, dst, send, recv, peer):
        return pltpu.make_async_remote_copy(
            src_ref=src, dst_ref=dst, send_sem=send, recv_sem=recv, device_id=peer, device_id_type=MESH
        )

    def lanes(c):
        return pl.ds(pl.multiple_of(c * LANES, LANES), LANES)

    def lat_copies(c):
        below = [
            remote(ref.at[2:8, :, lanes(c)], kv.at[c, i, 0:6], lat_s.at[c, i], lat_r.at[c, i], (down, lon))
            for i, ref in enumerate((k_ref, v_ref))
        ]
        above = [
            remote(ref.at[0:6, :, lanes(c)], kv.at[c, i, 14:20], lat_s.at[c, 2 + i], lat_r.at[c, 2 + i], (up, lon))
            for i, ref in enumerate((k_ref, v_ref))
        ]
        return below, above

    def edge_copies(c):
        return [
            remote(edge.at[c, 0], kv.at[c, :, LEFT + 3 : LEFT + 7], edge_s.at[c, 0], edge_r.at[c, 0], (lat, east)),
            remote(edge.at[c, 1], kv.at[c, :, RIGHT + 3 : RIGHT + 7], edge_s.at[c, 1], edge_r.at[c, 1], (lat, west)),
        ]

    def corner_copies(c):
        out = []
        for i, (base, peer) in enumerate(((LEFT, east), (RIGHT, west))):
            for j, first in enumerate((0, 7)):
                n = 2 * i + j
                out.append(
                    remote(
                        corner.at[c, i, j], kv.at[c, :, base + first : base + first + 3],
                        cor_s.at[c, n], cor_r.at[c, n], (lat, peer),
                    )
                )
        return out

    def gather_z(d):
        return remote(gath.at[lon], gath.at[lon], g_s.at[d], g_r.at[d], (lat, z_peers[d]))

    def gather_z_wait(d):
        return remote(gath.at[z_from[d]], gath.at[z_from[d]], g_s.at[d], g_r.at[d], (lat, z_peers[d]))

    def gather_y(d):
        return remote(gath.at[z_from[d]], gath.at[z_from[d]], gy_s.at[d], gy_r.at[d], (lat, y_peer))

    def gather_c(d):
        return remote(gath.at[z_from[d]], gath.at[z_from[d]], gc_s.at[d], gc_r.at[d], (lat, core_peer))

    def other_y(d):
        return lon_of(1 - why, (zed + ZN - d) % ZN, core)

    def gather_d(d):
        at = gath.at[other_y(d)]
        return remote(at, at, gd_s.at[d], gd_r.at[d], (lat, core_peer))

    def gather_y_wait(d):
        at = gath.at[other_y(d)]
        return remote(at, at, gy_s.at[d], gy_r.at[d], (lat, y_peer))

    def gather_c_wait(d):
        at = gath.at[lon_of(why, (zed + ZN - d) % ZN, 1 - core)]
        return remote(at, at, gc_s.at[d], gc_r.at[d], (lat, core_peer))

    def gather_d_wait(d):
        at = gath.at[lon_of(1 - why, (zed + ZN - d) % ZN, 1 - core)]
        return remote(at, at, gd_s.at[d], gd_r.at[d], (lat, core_peer))

    def side_copies(c):
        return [
            remote(side_out.at[c, 0], side_in.at[c, 0], side_s.at[c, 0], side_r.at[c, 0], (lat, west)),
            remote(side_out.at[c, 1], side_in.at[c, 1], side_s.at[c, 1], side_r.at[c, 1], (lat, east)),
        ]

    def grad_lat_copies(c):
        return [
            remote(lat_out.at[c, 0], lat_in.at[c, 0], glat_s.at[c, 0], glat_r.at[c, 0], (up, lon)),
            remote(lat_out.at[c, 1], lat_in.at[c, 1], glat_s.at[c, 1], glat_r.at[c, 1], (down, lon)),
        ]

    def zonal_core(c):
        return remote(z_out.at[c, 1 - core], z_in1.at[c], zc_s.at[c], zc_r.at[c], (lat, core_peer))

    def zonal_y(c):
        src = z_mid1.at[c, pl.ds((1 - why) * ZN, ZN)]
        return remote(src, z_in2.at[c], zy_s.at[c], zy_r.at[c], (lat, y_peer))

    def zonal_z(c, d):
        src = z_mid2.at[c, (zed + d) % ZN]
        return remote(src, z_in3.at[c, d], zz_s.at[c, d], zz_r.at[c, d], (lat, z_peers[d]))

    for i, ref in enumerate((k_ref, v_ref)):
        total = jnp.sum(ref[...].astype(F32), axis=1) * (COLS ** -0.5)
        if i == 0:
            pooled_keys = total
    gath[lon] = jnp.concatenate([pooled_keys, total], axis=0).astype(BF)

    def pack_edges(c):
        for i, ref in enumerate((k_ref, v_ref)):
            block = ref[:, :, lanes(c)].astype(F32)
            edge[c, 0, i] = block[:, 8:16].reshape(64, LANES).astype(BF).reshape(4, 16, LANES)
            edge[c, 1, i] = block[:, 0:8].reshape(64, LANES).astype(BF).reshape(4, 16, LANES)

    @pl.loop(0, CHUNKS)
    def _(c):
        pack_edges(c)

    pl.semaphore_wait(barrier, len(greeted))

    @pl.loop(0, CHUNKS)
    def _(c):
        below, above = lat_copies(c)

        @pl.when(lat < lats - 1)
        def _():
            for copy in below:
                copy.start()

        @pl.when(lat > 0)
        def _():
            for copy in above:
                copy.start()

    for d in (4, 3, 5, 2, 6, 1, 7):
        gather_z(d).start()
    gather_y(0).start()
    gather_c(0).start()

    @pl.loop(0, CHUNKS)
    def _(c):
        for copy in edge_copies(c):
            copy.start()

    @pl.loop(0, CHUNKS)
    def _(c):
        for i, ref in enumerate((k_ref, v_ref)):
            kv[c, i, 6:14] = ref[:, :, lanes(c)]

        @pl.when(lat == 0)
        def _():
            kv[c, :, 0:6] = jnp.zeros((2, 6, 16, LANES), BF)
            lat_in[c, 1] = jnp.zeros((2, 6, 16, LANES), BF)

        @pl.when(lat == lats - 1)
        def _():
            kv[c, :, 14:20] = jnp.zeros((2, 6, 16, LANES), BF)
            lat_in[c, 0] = jnp.zeros((2, 6, 16, LANES), BF)

    span_a = lax.broadcasted_iota(jnp.int32, (SPAN, 512), 0)
    lane_j = lax.broadcasted_iota(jnp.int32, (SPAN, 512), 1) // COLS
    select_a = ((REGION - 1 - lane_j) == span_a).astype(F32)
    centre = (lax.broadcasted_iota(jnp.int32, (SPAN, SPAN), 0) == RADIUS) & (
        lax.broadcasted_iota(jnp.int32, (SPAN, SPAN), 1) == RADIUS
    )
    sub = lax.broadcasted_iota(jnp.int32, (32, 512), 0)
    place = jnp.where(sub < 16, sub, jnp.where(sub < 24, sub - 24, sub - 8))
    offset = place - lax.broadcasted_iota(jnp.int32, (32, 512), 1) % COLS + RADIUS
    top_open = jnp.where(lat > 0, 0.0, NEVER).astype(F32)
    low_open = jnp.where(lat < lats - 1, 0.0, NEVER).astype(F32)

    def build_mask(pair):
        for half in range(2):
            head = near_ref[pair * 2 + half]
            allowed = jnp.where((head == 1) | centre, 1.0, 0.0).astype(F32)
            by_lane = lax.dot_general(
                allowed, select_a, (((0,), (0,)), ((), ())), preferred_element_type=F32
            )
            full = jnp.full((32, 512), NEVER, F32)
            by_lane = (by_lane - 1.0) * (-NEVER)
            for b in range(SPAN):
                full = jnp.where(offset == b, by_lane[b : b + 1, :], full)
            wide[...] = full
            for row in range(REGION):
                start = (REGION - 1 - row) * COLS
                tile, phase = start // 128, start % 128
                if phase:
                    both = wide[:, tile * 128 : tile * 128 + 256]
                    part = pltpu.roll(both, 256 - phase, 1)[:, 0:128]
                else:
                    part = wide[:, tile * 128 : tile * 128 + 128]
                if row < RADIUS:
                    part = jnp.minimum(part, top_open)
                if row >= ROWS + RADIUS:
                    part = jnp.minimum(part, low_open)
                at = slice(half * 128, half * 128 + 128)
                bias[pair, row * 16 : row * 16 + 16, at] = part[0:16]
                bias[pair, 320 + row * 8 : 328 + row * 8, at] = part[16:24]
                bias[pair, 480 + row * 8 : 488 + row * 8, at] = part[24:32]

    @pl.loop(0, 4)
    def _(pair):
        build_mask(pair)

    for d in (1, 7, 2, 6, 3, 5, 4):
        gather_z_wait(d).wait_recv()
        gather_y(d).start()
        gather_c(d).start()

    @pl.loop(4, 8)
    def _(pair):
        build_mask(pair)

    row_of_lane = lax.broadcasted_iota(jnp.int32, (ROWS, 128), 1) // COLS
    row_hot = (row_of_lane == lax.broadcasted_iota(jnp.int32, (ROWS, 128), 0)).astype(F32)
    zonal_ok = jnp.where(zonal_ref[...] == 1, 1.0, 0.0).astype(F32)
    by_sector = lax.dot_general(zonal_ok, row_hot, (((0,), (0,)), ((), ())), preferred_element_type=F32)
    for s in range(SECT):
        bias_z[s * 8 : s * 8 + 8, :] = (by_sector[s : s + 1, :] * row_hot - 1.0) * (-NEVER)

    @pl.loop(0, CHUNKS)
    def _(c):
        below, above = lat_copies(c)

        @pl.when(lat > 0)
        def _():
            for copy in below:
                copy.wait_recv()

        @pl.when(lat < lats - 1)
        def _():
            for copy in above:
                copy.wait_recv()

        for i in range(2):
            for j, first in enumerate((0, 14)):
                block = kv[c, i, first : first + 6].astype(F32)
                corner[c, 0, j, i] = block[:, 8:16].reshape(48, LANES).astype(BF).reshape(3, 16, LANES)
                corner[c, 1, j, i] = block[:, 0:8].reshape(48, LANES).astype(BF).reshape(3, 16, LANES)
        for copy in corner_copies(c):
            copy.start()

    for d in (0, 1, 7, 2, 6, 3, 5, 4):
        gather_y_wait(d).wait_recv()
        gather_d(d).start()
    for d in range(ZN):
        gather_c_wait(d).wait_recv()
    for d in range(ZN):
        gather_d_wait(d).wait_recv()

    low_half = lax.broadcasted_iota(jnp.int32, (128, 128), 1) < 64

    def split_pair(block):
        zero = jnp.zeros_like(block)
        both = jnp.concatenate([jnp.where(low_half, block, zero), jnp.where(low_half, zero, block)], axis=0)
        return both.astype(BF)

    def own_heads(product):
        return jnp.concatenate([product[0:64, 0:128], product[64:128, 128:256]], axis=0)

    NT = (((1,), (1,)), ((), ()))
    NN = (((1,), (0,)), ((), ()))
    TN = (((0,), (0,)), ((), ()))
    STEPS = TILES // 8

    def attend(c, half):
        here = pl.ds(pl.multiple_of(half * 128, 128), 128)
        there = pl.ds(pl.multiple_of(c * LANES + half * 128, 128), 128)
        pair = c * 2 + half
        q_both = split_pair(q_ref[:, :, there].reshape(128, 128).astype(F32) * 0.125)
        grad = do_ref[:, :, there].reshape(128, 128).astype(F32)
        grad_both = split_pair(grad)

        def tokens(i, t):
            return kv[c, i, t * 8 : t * 8 + 8, :, here].reshape(128, 128)

        highest = jnp.full((8, 256), NEVER, F32)
        for t in range(STEPS):
            s = lax.dot_general(tokens(0, t), q_both, NT, preferred_element_type=F32)
            if t < 5:
                s = s + bias[pair, t * 128 : t * 128 + 128, :]
            else:
                z = bias_z[(t - 5) * 128 : (t - 4) * 128, :]
                s = s + jnp.concatenate([z, z], axis=1)
            scores[t * 128 : t * 128 + 128, :] = s
            highest = jnp.maximum(highest, jnp.max(s.reshape(16, 8, 256), axis=0))
        top = jnp.max(highest, axis=0, keepdims=True)
        total = jnp.zeros((8, 256), F32)
        for t in range(STEPS):
            e = jnp.exp(scores[t * 128 : t * 128 + 128, :] - top)
            scores[t * 128 : t * 128 + 128, :] = e
            total = total + jnp.sum(e.reshape(16, 8, 256), axis=0)
        inverse = 1.0 / jnp.sum(total, axis=0, keepdims=True)
        out = jnp.zeros((128, 256), F32)
        for t in range(STEPS):
            p = scores[t * 128 : t * 128 + 128, :] * inverse
            scores[t * 128 : t * 128 + 128, :] = p
            p = p.astype(BF)
            probs[t * 128 : t * 128 + 128, :] = p
            out = out + lax.dot_general(tokens(1, t), p, TN, preferred_element_type=F32)
        out = own_heads(out)
        att_ref[:, :, there] = out.T.astype(BF).reshape(8, 16, 128)
        prod = out * grad.T
        delta = jnp.concatenate(
            [jnp.sum(prod[0:64], axis=0, keepdims=True), jnp.sum(prod[64:128], axis=0, keepdims=True)], axis=1
        )
        grad_q = jnp.zeros((128, 256), F32)
        for t in range(STEPS):
            dp = lax.dot_general(tokens(1, t), grad_both, NT, preferred_element_type=F32)
            ds = (scores[t * 128 : t * 128 + 128, :] * (dp - delta)).astype(BF)
            grad_q = grad_q + lax.dot_general(tokens(0, t), ds, TN, preferred_element_type=F32)
            dk = lax.dot_general(ds, q_both, NN, preferred_element_type=F32)
            dv = lax.dot_general(probs[t * 128 : t * 128 + 128, :], grad_both, NN, preferred_element_type=F32)
            if t < 5:
                for i, d in enumerate((dk, dv)):
                    d = d.reshape(8, 16, 128)
                    for n, (lo, hi) in enumerate(((CENTRE, LEFT), (LEFT, RIGHT), (RIGHT, ZONAL))):
                        first, last = max(lo, t * 8), min(hi, t * 8 + 8)
                        if first >= last:
                            continue
                        piece = d[first - t * 8 : last - t * 8]
                        if n == 0:
                            acc[c, i, first:last, :, here] = piece
                        else:
                            side_out[c, n - 1, i, first - lo : last - lo, :, here] = piece.astype(BF)
            else:
                both = jnp.concatenate([dk.reshape(16, 8, 128), dv.reshape(16, 8, 128)], axis=1)
                both = both.astype(BF).reshape(8, 2, 16, 128)
                for n in range(2):
                    z_out[c, n, (t - 5) * 8 : (t - 4) * 8, :, here] = both[:, n]
        grad_q = own_heads(grad_q) * 0.125
        gq_ref[:, :, there] = grad_q.T.astype(BF).reshape(8, 16, 128)

    def stage1(c):
        block = gath[:, :, lanes(c)].astype(F32)
        for i in range(2):
            rows = block[:, i * 8 : i * 8 + 8].reshape(SECT * 8, LANES).astype(BF)
            kv[c, i, ZONAL:TILES] = rows.reshape(16, 16, LANES)
        for copy in edge_copies(c) + corner_copies(c):
            copy.wait_recv()

        @pl.loop(0, 2)
        def _(half):
            attend(c, half)

        for copy in side_copies(c):
            copy.start()
        zonal_core(c).start()

    def stage2(c):
        for copy in side_copies(c):
            copy.wait_recv()
        for i in range(2):
            from_east = side_in[c, 0, i].astype(F32).reshape(REGION, 8, LANES)
            from_west = side_in[c, 1, i].astype(F32).reshape(REGION, 8, LANES)
            total = acc[c, i] + jnp.concatenate([from_west, from_east], axis=1)
            acc[c, i, 6:14] = total[6:14]
            lat_out[c, 0, i] = total[0:6].astype(BF)
            lat_out[c, 1, i] = total[14:20].astype(BF)
        to_up, to_down = grad_lat_copies(c)

        @pl.when(lat > 0)
        def _():
            to_up.start()

        @pl.when(lat < lats - 1)
        def _():
            to_down.start()

        zonal_core(c).wait_recv()
        z_mid1[c] = (z_out[c, core].astype(F32) + z_in1[c].astype(F32)).astype(BF)
        zonal_y(c).start()

    def stage3(c):
        zonal_y(c).wait_recv()
        z_mid2[c] = (z_mid1[c, pl.ds(why * ZN, ZN)].astype(F32) + z_in2[c].astype(F32)).astype(BF)
        for d in (4, 3, 5, 2, 6, 1, 7):
            zonal_z(c, d).start()

    def stage4(c):
        total = z_mid2[c, zed].astype(F32)
        for d in (1, 7, 2, 6, 3, 5, 4):
            zonal_z(c, d).wait_recv()
            total = total + z_in3[c, d].astype(F32)
        total = total * (COLS ** -0.5)
        to_up, to_down = grad_lat_copies(c)

        @pl.when(lat < lats - 1)
        def _():
            to_up.wait_recv()

        @pl.when(lat > 0)
        def _():
            to_down.wait_recv()

        for i, ref in enumerate((gk_ref, gv_ref)):
            for r in range(ROWS):
                row = acc[c, i, 6 + r] + total[i * 8 + r : i * 8 + r + 1, :]
                if r >= 2:
                    row = row + lat_in[c, 0, i, r - 2].astype(F32)
                if r < 6:
                    row = row + lat_in[c, 1, i, r].astype(F32)
                ref[r, :, lanes(c)] = row.astype(BF)

    @pl.loop(0, CHUNKS + 3)
    def _(step):
        @pl.when(step < CHUNKS)
        def _():
            stage1(step)

        @pl.when((step >= 1) & (step < CHUNKS + 1))
        def _():
            stage2(step - 1)

        @pl.when((step >= 2) & (step < CHUNKS + 2))
        def _():
            stage3(step - 2)

        @pl.when(step >= 3)
        def _():
            stage4(step - 3)

    @pl.loop(0, CHUNKS)
    def _(c):
        below, above = lat_copies(c)
        to_up, to_down = grad_lat_copies(c)

        @pl.when(lat < lats - 1)
        def _():
            for copy in below + [to_down]:
                copy.wait_send()

        @pl.when(lat > 0)
        def _():
            for copy in above + [to_up]:
                copy.wait_send()

        for copy in edge_copies(c) + corner_copies(c) + side_copies(c) + [zonal_core(c), zonal_y(c)]:
            copy.wait_send()
        for d in range(1, ZN):
            zonal_z(c, d).wait_send()

    for d in range(ZN):
        if d > 0:
            gather_z(d).wait_send()
        gather_y(d).wait_send()
        gather_c(d).wait_send()
        gather_d(d).wait_send()


def body(queries, keys, values, cotangent, near_pattern, zonal_pattern):
    block = jax.ShapeDtypeStruct(queries.shape, BF)
    dma = pltpu.SemaphoreType.DMA
    vm = pltpu.VMEM
    scratch = [
        vm((CHUNKS, 2, TILES, 16, LANES), BF),
        vm((CHUNKS, 2, 2, 4, 16, LANES), BF),
        vm((CHUNKS, 2, 2, 2, 3, 16, LANES), BF),
        vm((SECT, 16, 1024), BF),
        vm((8, 640, 256), F32),
        vm((SECT * 8, 128), F32),
        vm((32, 512), F32),
        vm((TILES * 16, 256), F32),
        vm((TILES * 16, 256), BF),
        vm((CHUNKS, 2, REGION, 16, LANES), F32),
        vm((CHUNKS, 2, 2, 10, 16, LANES), BF),
        vm((CHUNKS, 2, 2, 10, 16, LANES), BF),
        vm((CHUNKS, 2, 2, 6, 16, LANES), BF),
        vm((CHUNKS, 2, 2, 6, 16, LANES), BF),
        vm((CHUNKS, 2, 16, 16, LANES), BF),
        vm((CHUNKS, 16, 16, LANES), BF),
        vm((CHUNKS, 16, 16, LANES), BF),
        vm((CHUNKS, 8, 16, LANES), BF),
        vm((CHUNKS, 8, 16, LANES), BF),
        vm((CHUNKS, 8, 16, LANES), BF),
    ]
    sems = [(CHUNKS, 4), (CHUNKS, 2), (CHUNKS, 4), (ZN,), (ZN,), (ZN,), (ZN,), (CHUNKS, 2), (CHUNKS, 2), (CHUNKS,), (CHUNKS,), (CHUNKS, ZN)]
    for shape in sems:
        scratch += [dma(shape), dma(shape)]
    return pl.pallas_call(
        kernel,
        out_shape=[block] * 4,
        in_specs=[pl.BlockSpec(memory_space=pltpu.VMEM)] * 6,
        out_specs=[pl.BlockSpec(memory_space=pltpu.VMEM)] * 4,
        scratch_shapes=scratch,
        compiler_params=pltpu.CompilerParams(
            collective_id=0, has_side_effects=True, vmem_limit_bytes=56 * 1024 * 1024
        ),
        cost_estimate=pl.CostEstimate(flops=3_000_000_000, bytes_accessed=2 << 20, transcendentals=1 << 20),
    )(queries, keys, values, cotangent, near_pattern, zonal_pattern)


def solution(mesh):
    grid = P("lat", "lon", None)
    return jax.shard_map(
        body,
        mesh=mesh,
        in_specs=(grid, grid, grid, grid, P(), P("lat", None)),
        out_specs=(grid, grid, grid, grid),
        check_vma=False,
    )
```

```python
import jax
import jax.numpy as jnp
from jax import lax
from jax.experimental import pallas as pl
from jax.experimental.pallas import tpu as pltpu
from jax.sharding import PartitionSpec as P

MESH = pl.DeviceIdType.MESH
RADIUS = 6
SPAN = 2 * RADIUS + 1
ROWS = 8
COLS = 16
REGION = ROWS + 2 * RADIUS
SECT = 32
ZN = 8
LANES = 256
CHUNKS = 4
TILES = 56
CENTRE, LEFT, RIGHT, ZONAL = 0, 20, 30, 40
NEVER = -1e30
BF, F32 = jnp.bfloat16, jnp.float32


def kernel(
    q_ref, k_ref, v_ref, do_ref, near_ref, zonal_ref,
    att_ref, gq_ref, gk_ref, gv_ref,
    kv, edge, corner, gath, bias, bias_z, wide, scores, probs,
    acc, side_out, side_in, lat_out, lat_in,
    z_out, z_in1, z_mid1, z_in2, z_mid2, z_in3,
    relay, relay_g, rel_s, rel_r, fwd_s, fwd_r, relg_s, relg_r, fwdg_s, fwdg_r,
    lat_s, lat_r, edge_s, edge_r, cor_s, cor_r,
    g_s, g_r, gy_s, gy_r, gc_s, gc_r,
    side_s, side_r, glat_s, glat_r, zc_s, zc_r, zy_s, zy_r, zz_s, zz_r,
):
    lat, lon = lax.axis_index("lat"), lax.axis_index("lon")
    lats, lons = lax.axis_size("lat"), lax.axis_size("lon")
    core, zed, why = lon % 2, (lon // 2) % ZN, lon // (2 * ZN)

    def lon_of(y, z, c):
        return (y * ZN + z) * 2 + c

    up, down = (lat + lats - 1) % lats, (lat + 1) % lats
    west, east = (lon + lons - 1) % lons, (lon + 1) % lons
    core_peer = lon_of(why, zed, 1 - core)
    y_peer = lon_of(1 - why, zed, core)
    z_peers = [None] + [lon_of(why, (zed + d) % ZN, core) for d in range(1, ZN)]

    barrier = pltpu.get_barrier_semaphore()
    greeted = [(up, lon), (down, lon), (lat, west), (lat, east), (lat, core_peer), (lat, y_peer)]
    greeted += [(lat, peer) for peer in z_peers[1:]]
    for peer in greeted:
        pl.semaphore_signal(barrier, inc=1, device_id=peer, device_id_type=MESH)

    middle = lats // 2
    crosses = (lat == middle - 1) | (lat == middle)
    far_down, far_up = lat == middle - 1, lat == middle

    @pl.when(far_down)
    def _():
        pl.semaphore_signal(barrier, inc=1, device_id=(down, y_peer), device_id_type=MESH)

    @pl.when(far_up)
    def _():
        pl.semaphore_signal(barrier, inc=1, device_id=(up, y_peer), device_id_type=MESH)

    def remote(src, dst, send, recv, peer):
        return pltpu.make_async_remote_copy(
            src_ref=src, dst_ref=dst, send_sem=send, recv_sem=recv, device_id=peer, device_id_type=MESH
        )

    def lanes(c):
        return pl.ds(pl.multiple_of(c * LANES, LANES), LANES)

    def lat_copies(c):
        below = [
            remote(ref.at[2:8, :, lanes(c)], kv.at[c, i, 0:6], lat_s.at[c, i], lat_r.at[c, i], (down, lon))
            for i, ref in enumerate((k_ref, v_ref))
        ]
        above = [
            remote(ref.at[0:6, :, lanes(c)], kv.at[c, i, 14:20], lat_s.at[c, 2 + i], lat_r.at[c, 2 + i], (up, lon))
            for i, ref in enumerate((k_ref, v_ref))
        ]
        return below, above

    def cross_copies(c):
        below = [
            remote(ref.at[2:8, :, lanes(c)], relay.at[c, i], lat_s.at[c, i], rel_r.at[c, i], (down, y_peer))
            for i, ref in enumerate((k_ref, v_ref))
        ]
        above = [
            remote(ref.at[0:6, :, lanes(c)], relay.at[c, i], lat_s.at[c, 2 + i], rel_r.at[c, i], (up, y_peer))
            for i, ref in enumerate((k_ref, v_ref))
        ]
        return below, above

    def pass_on(c):
        at = kv.at[c, :, pl.ds((middle - lat) * (REGION - 6), 6)]
        return remote(relay.at[c], at, fwd_s.at[c], fwd_r.at[c], (lat, y_peer))

    def cross_grads(c):
        return [
            remote(lat_out.at[c, 0], relay_g.at[c], glat_s.at[c, 0], relg_r.at[c], (up, y_peer)),
            remote(lat_out.at[c, 1], relay_g.at[c], glat_s.at[c, 1], relg_r.at[c], (down, y_peer)),
        ]

    def pass_on_grads(c):
        at = lat_in.at[c, lat - middle + 1]
        return remote(relay_g.at[c], at, fwdg_s.at[c], fwdg_r.at[c], (lat, y_peer))

    def edge_copies(c):
        return [
            remote(edge.at[c, 0], kv.at[c, :, LEFT + 3 : LEFT + 7], edge_s.at[c, 0], edge_r.at[c, 0], (lat, east)),
            remote(edge.at[c, 1], kv.at[c, :, RIGHT + 3 : RIGHT + 7], edge_s.at[c, 1], edge_r.at[c, 1], (lat, west)),
        ]

    def corner_copies(c):
        out = []
        for i, (base, peer) in enumerate(((LEFT, east), (RIGHT, west))):
            for j, first in enumerate((0, 7)):
                n = 2 * i + j
                out.append(
                    remote(
                        corner.at[c, i, j], kv.at[c, :, base + first : base + first + 3],
                        cor_s.at[c, n], cor_r.at[c, n], (lat, peer),
                    )
                )
        return out

    def gather_y(y):
        at = gath.at[:, core, y, zed]
        return remote(at, at, gy_s.at[0], gy_r.at[0], (lat, y_peer))

    def gather_z(c, d):
        at = gath.at[c, core, :, zed]
        return remote(at, at, g_s.at[c, d], g_r.at[c, d], (lat, z_peers[d]))

    def gather_z_wait(c, d):
        at = gath.at[c, core, :, (zed + ZN - d) % ZN]
        return remote(at, at, g_s.at[c, d], g_r.at[c, d], (lat, z_peers[d]))

    def gather_c(c, which):
        at = gath.at[c, which]
        return remote(at, at, gc_s.at[c], gc_r.at[c], (lat, core_peer))

    def side_copies(c):
        return [
            remote(side_out.at[c, 0], side_in.at[c, 0], side_s.at[c, 0], side_r.at[c, 0], (lat, west)),
            remote(side_out.at[c, 1], side_in.at[c, 1], side_s.at[c, 1], side_r.at[c, 1], (lat, east)),
        ]

    def grad_lat_copies(c):
        return [
            remote(lat_out.at[c, 0], lat_in.at[c, 0], glat_s.at[c, 0], glat_r.at[c, 0], (up, lon)),
            remote(lat_out.at[c, 1], lat_in.at[c, 1], glat_s.at[c, 1], glat_r.at[c, 1], (down, lon)),
        ]

    def zonal_core(c):
        return remote(z_out.at[c, 1 - core], z_in1.at[c], zc_s.at[c], zc_r.at[c], (lat, core_peer))

    def zonal_y(c):
        src = z_mid1.at[c, pl.ds((1 - why) * ZN, ZN)]
        return remote(src, z_in2.at[c], zy_s.at[c], zy_r.at[c], (lat, y_peer))

    def zonal_z(c, d):
        src = z_mid2.at[c, (zed + d) % ZN]
        return remote(src, z_in3.at[c, d], zz_s.at[c, d], zz_r.at[c, d], (lat, z_peers[d]))

    for i, ref in enumerate((k_ref, v_ref)):
        total = jnp.sum(ref[...].astype(F32), axis=1) * (COLS ** -0.5)
        if i == 0:
            pooled_keys = total
    pooled = jnp.concatenate([pooled_keys, total], axis=0).astype(BF)
    for c in range(CHUNKS):
        gath[c, core, why, zed] = pooled[:, c * LANES : (c + 1) * LANES]

    def pack_edges(c):
        for i, ref in enumerate((k_ref, v_ref)):
            block = ref[:, :, lanes(c)].astype(F32)
            edge[c, 0, i] = block[:, 8:16].reshape(64, LANES).astype(BF).reshape(4, 16, LANES)
            edge[c, 1, i] = block[:, 0:8].reshape(64, LANES).astype(BF).reshape(4, 16, LANES)

    @pl.loop(0, CHUNKS)
    def _(c):
        pack_edges(c)

    pl.semaphore_wait(barrier, len(greeted) + jnp.where(crosses, 1, 0))

    def send_rows(c):
        below, above = lat_copies(c)
        far_below, far_above = cross_copies(c)
        near = c == 0

        @pl.when((lat < lats - 1) & ((lat != middle - 1) | near))
        def _():
            for copy in below:
                copy.start()

        @pl.when(far_down & (not near))
        def _():
            for copy in far_below:
                copy.start()

        @pl.when((lat > 0) & ((lat != middle) | near))
        def _():
            for copy in above:
                copy.start()

        @pl.when(far_up & (not near))
        def _():
            for copy in far_above:
                copy.start()

    def send(c):
        for copy in edge_copies(c):
            copy.start()

    def send_pooled(c):
        for d in (4, 3, 5, 2, 6, 1, 7):
            gather_z(c, d).start()

    gather_y(why).start()
    send_rows(0)
    send(0)
    for c in range(1, CHUNKS):
        send_rows(c)

    @pl.loop(0, CHUNKS)
    def _(c):
        for i, ref in enumerate((k_ref, v_ref)):
            kv[c, i, 6:14] = ref[:, :, lanes(c)]

        @pl.when(lat == 0)
        def _():
            kv[c, :, 0:6] = jnp.zeros((2, 6, 16, LANES), BF)
            lat_in[c, 1] = jnp.zeros((2, 6, 16, LANES), BF)

        @pl.when(lat == lats - 1)
        def _():
            kv[c, :, 14:20] = jnp.zeros((2, 6, 16, LANES), BF)
            lat_in[c, 0] = jnp.zeros((2, 6, 16, LANES), BF)

    span_a = lax.broadcasted_iota(jnp.int32, (SPAN, 512), 0)
    lane_j = lax.broadcasted_iota(jnp.int32, (SPAN, 512), 1) // COLS
    select_a = ((REGION - 1 - lane_j) == span_a).astype(F32)
    centre = (lax.broadcasted_iota(jnp.int32, (SPAN, SPAN), 0) == RADIUS) & (
        lax.broadcasted_iota(jnp.int32, (SPAN, SPAN), 1) == RADIUS
    )
    sub = lax.broadcasted_iota(jnp.int32, (32, 512), 0)
    place = jnp.where(sub < 16, sub, jnp.where(sub < 24, sub - 24, sub - 8))
    offset = place - lax.broadcasted_iota(jnp.int32, (32, 512), 1) % COLS + RADIUS
    top_open = jnp.where(lat > 0, 0.0, NEVER).astype(F32)
    low_open = jnp.where(lat < lats - 1, 0.0, NEVER).astype(F32)

    def build_mask(pair):
        for half in range(2):
            head = near_ref[pair * 2 + half]
            allowed = jnp.where((head == 1) | centre, 1.0, 0.0).astype(F32)
            by_lane = lax.dot_general(
                allowed, select_a, (((0,), (0,)), ((), ())), preferred_element_type=F32
            )
            full = jnp.full((32, 512), NEVER, F32)
            by_lane = (by_lane - 1.0) * (-NEVER)
            for b in range(SPAN):
                full = jnp.where(offset == b, by_lane[b : b + 1, :], full)
            wide[...] = full
            for row in range(REGION):
                start = (REGION - 1 - row) * COLS
                tile, phase = start // 128, start % 128
                if phase:
                    both = wide[:, tile * 128 : tile * 128 + 256]
                    part = pltpu.roll(both, 256 - phase, 1)[:, 0:128]
                else:
                    part = wide[:, tile * 128 : tile * 128 + 128]
                if row < RADIUS:
                    part = jnp.minimum(part, top_open)
                if row >= ROWS + RADIUS:
                    part = jnp.minimum(part, low_open)
                at = slice(half * 128, half * 128 + 128)
                bias[pair, row * 16 : row * 16 + 16, at] = part[0:16]
                bias[pair, 320 + row * 8 : 328 + row * 8, at] = part[16:24]
                bias[pair, 480 + row * 8 : 488 + row * 8, at] = part[24:32]

    row_of_lane = lax.broadcasted_iota(jnp.int32, (ROWS, 128), 1) // COLS
    row_hot = (row_of_lane == lax.broadcasted_iota(jnp.int32, (ROWS, 128), 0)).astype(F32)

    def build_zonal_mask():
        zonal_ok = jnp.where(zonal_ref[...] == 1, 1.0, 0.0).astype(F32)
        by_sector = lax.dot_general(zonal_ok, row_hot, (((0,), (0,)), ((), ())), preferred_element_type=F32)
        for n in range(SECT):
            s = n % 16 * 2 + n // 16
            bias_z[n * 8 : n * 8 + 8, :] = (by_sector[s : s + 1, :] * row_hot - 1.0) * (-NEVER)

    def relay_rows(c):
        @pl.when(crosses)
        def _():
            for copy in cross_copies(c)[0]:
                copy.wait_recv()
            pass_on(c).start()

    def prepare_a(c):
        below, above = lat_copies(c)
        near = c == 0

        @pl.when((lat > 0) & ((lat != middle) | near))
        def _():
            for copy in below:
                copy.wait_recv()

        @pl.when((lat < lats - 1) & ((lat != middle - 1) | near))
        def _():
            for copy in above:
                copy.wait_recv()

        @pl.when(crosses & jnp.logical_not(near))
        def _():
            pass_on(c).wait_recv()

        for i in range(2):
            for j, first in enumerate((0, 14)):
                block = kv[c, i, first : first + 6].astype(F32)
                corner[c, 0, j, i] = block[:, 8:16].reshape(48, LANES).astype(BF).reshape(3, 16, LANES)
                corner[c, 1, j, i] = block[:, 0:8].reshape(48, LANES).astype(BF).reshape(3, 16, LANES)
        for copy in corner_copies(c):
            copy.start()

    def prepare_b(c):
        for d in range(1, ZN):
            gather_z_wait(c, d).wait_recv()
        gather_c(c, core).start()

    def build_masks(first, last):
        @pl.loop(first, last)
        def _(pair):
            build_mask(pair)

    build_masks(0, 4)
    gather_y(1 - why).wait_recv()
    send_pooled(0)
    send(1)
    build_zonal_mask()
    build_masks(4, 8)
    prepare_a(0)
    send_pooled(1)
    send(2)
    relay_rows(1)
    prepare_b(0)
    relay_rows(2)
    send(3)
    prepare_a(1)

    low_half = lax.broadcasted_iota(jnp.int32, (128, 128), 1) < 64

    def split_pair(block):
        zero = jnp.zeros_like(block)
        both = jnp.concatenate([jnp.where(low_half, block, zero), jnp.where(low_half, zero, block)], axis=0)
        return both.astype(BF)

    def own_heads(product):
        return jnp.concatenate([product[0:64, 0:128], product[64:128, 128:256]], axis=0)

    NT = (((1,), (1,)), ((), ()))
    NN = (((1,), (0,)), ((), ()))
    TN = (((0,), (0,)), ((), ()))
    STEPS = TILES // 8

    def attend(c, half):
        here = pl.ds(pl.multiple_of(half * 128, 128), 128)
        there = pl.ds(pl.multiple_of(c * LANES + half * 128, 128), 128)
        pair = c * 2 + half
        q_both = split_pair(q_ref[:, :, there].reshape(128, 128).astype(F32) * 0.125)
        grad = do_ref[:, :, there].reshape(128, 128).astype(F32)
        grad_both = split_pair(grad)

        def tokens(i, t):
            return kv[c, i, t * 8 : t * 8 + 8, :, here].reshape(128, 128)

        highest = jnp.full((8, 256), NEVER, F32)
        for t in range(STEPS):
            s = lax.dot_general(tokens(0, t), q_both, NT, preferred_element_type=F32)
            if t < 5:
                s = s + bias[pair, t * 128 : t * 128 + 128, :]
            else:
                z = bias_z[(t - 5) * 128 : (t - 4) * 128, :]
                s = s + jnp.concatenate([z, z], axis=1)
            scores[t * 128 : t * 128 + 128, :] = s
            highest = jnp.maximum(highest, jnp.max(s.reshape(16, 8, 256), axis=0))
        top = jnp.max(highest, axis=0, keepdims=True)
        total = jnp.zeros((8, 256), F32)
        for t in range(STEPS):
            e = jnp.exp(scores[t * 128 : t * 128 + 128, :] - top)
            scores[t * 128 : t * 128 + 128, :] = e
            total = total + jnp.sum(e.reshape(16, 8, 256), axis=0)
        inverse = 1.0 / jnp.sum(total, axis=0, keepdims=True)
        out = jnp.zeros((128, 256), F32)
        for t in range(STEPS):
            p = scores[t * 128 : t * 128 + 128, :] * inverse
            scores[t * 128 : t * 128 + 128, :] = p
            p = p.astype(BF)
            probs[t * 128 : t * 128 + 128, :] = p
            out = out + lax.dot_general(tokens(1, t), p, TN, preferred_element_type=F32)
        out = own_heads(out)
        att_ref[:, :, there] = out.T.astype(BF).reshape(8, 16, 128)
        prod = out * grad.T
        delta = jnp.concatenate(
            [jnp.sum(prod[0:64], axis=0, keepdims=True), jnp.sum(prod[64:128], axis=0, keepdims=True)], axis=1
        )
        grad_q = jnp.zeros((128, 256), F32)
        for t in range(STEPS):
            dp = lax.dot_general(tokens(1, t), grad_both, NT, preferred_element_type=F32)
            ds = (scores[t * 128 : t * 128 + 128, :] * (dp - delta)).astype(BF)
            grad_q = grad_q + lax.dot_general(tokens(0, t), ds, TN, preferred_element_type=F32)
            dk = lax.dot_general(ds, q_both, NN, preferred_element_type=F32)
            dv = lax.dot_general(probs[t * 128 : t * 128 + 128, :], grad_both, NN, preferred_element_type=F32)
            if t < 5:
                for i, d in enumerate((dk, dv)):
                    d = d.reshape(8, 16, 128)
                    for n, (lo, hi) in enumerate(((CENTRE, LEFT), (LEFT, RIGHT), (RIGHT, ZONAL))):
                        first, last = max(lo, t * 8), min(hi, t * 8 + 8)
                        if first >= last:
                            continue
                        piece = d[first - t * 8 : last - t * 8]
                        if n == 0:
                            acc[c, i, first:last, :, here] = piece
                        else:
                            side_out[c, n - 1, i, first - lo : last - lo, :, here] = piece.astype(BF)
            else:
                both = jnp.concatenate([dk.reshape(16, 8, 128), dv.reshape(16, 8, 128)], axis=1)
                z_out[c, t - 5, :, :, here] = both.astype(BF)
        grad_q = own_heads(grad_q) * 0.125
        gq_ref[:, :, there] = grad_q.T.astype(BF).reshape(8, 16, 128)

    def load(c):
        gather_c(c, 1 - core).wait_recv()
        for first in range(2):
            block = gath[c, first].reshape(16, 16, LANES).astype(F32)
            for i in range(2):
                rows = block[:, i * 8 : i * 8 + 8].reshape(128, LANES).astype(BF)
                kv[c, i, ZONAL + first * 8 : ZONAL + first * 8 + 8] = rows.reshape(8, 16, LANES)
        for copy in edge_copies(c) + corner_copies(c):
            copy.wait_recv()

    def stage1(c):
        zonal_core(c).start()
        for copy in side_copies(c):
            copy.start()

    def stage2_zonal(c):
        zonal_core(c).wait_recv()
        z_mid1[c] = (z_out[c, core].astype(F32) + z_in1[c].astype(F32)).astype(BF)
        zonal_y(c).start()

    def stage2_side(c):
        for copy in side_copies(c):
            copy.wait_recv()
        for i in range(2):
            from_east = side_in[c, 0, i].astype(F32).reshape(REGION, 8, LANES)
            from_west = side_in[c, 1, i].astype(F32).reshape(REGION, 8, LANES)
            total = acc[c, i] + jnp.concatenate([from_west, from_east], axis=1)
            acc[c, i, 6:14] = total[6:14]
            lat_out[c, 0, i] = total[0:6].astype(BF)
            lat_out[c, 1, i] = total[14:20].astype(BF)
        to_up, to_down = grad_lat_copies(c)
        far_to_up, far_to_down = cross_grads(c)
        near = c == CHUNKS - 1

        @pl.when((lat > 0) & ((lat != middle) | near))
        def _():
            to_up.start()

        @pl.when(far_up & jnp.logical_not(near))
        def _():
            far_to_up.start()

        @pl.when((lat < lats - 1) & ((lat != middle - 1) | near))
        def _():
            to_down.start()

        @pl.when(far_down & jnp.logical_not(near))
        def _():
            far_to_down.start()

    def relay_grads(c):
        @pl.when(crosses)
        def _():
            cross_grads(c)[0].wait_recv()
            pass_on_grads(c).start()

    def stage3(c):
        zonal_y(c).wait_recv()
        z_mid2[c] = (z_mid1[c, pl.ds(why * ZN, ZN)].astype(F32) + z_in2[c].astype(F32)).astype(BF)
        for d in (4, 3, 5, 2, 6, 1, 7):
            zonal_z(c, d).start()

    def stage4(c):
        total = z_mid2[c, zed].astype(F32)
        for d in (1, 7, 2, 6, 3, 5, 4):
            zonal_z(c, d).wait_recv()
            total = total + z_in3[c, d].astype(F32)
        total = total * (COLS ** -0.5)
        to_up, to_down = grad_lat_copies(c)
        near = c == CHUNKS - 1

        @pl.when((lat < lats - 1) & ((lat != middle - 1) | near))
        def _():
            to_up.wait_recv()

        @pl.when((lat > 0) & ((lat != middle) | near))
        def _():
            to_down.wait_recv()

        @pl.when(crosses & jnp.logical_not(near))
        def _():
            pass_on_grads(c).wait_recv()

        for i, ref in enumerate((gk_ref, gv_ref)):
            for r in range(ROWS):
                row = acc[c, i, 6 + r] + total[i * 8 + r : i * 8 + r + 1, :]
                if r >= 2:
                    row = row + lat_in[c, 0, i, r - 2].astype(F32)
                if r < 6:
                    row = row + lat_in[c, 1, i, r].astype(F32)
                ref[r, :, lanes(c)] = row.astype(BF)

    @pl.loop(0, CHUNKS)
    def _(c):
        load(c)

        @pl.when(c == 0)
        def _():
            relay_rows(3)

        attend(c, 0)

        @pl.when(c < CHUNKS - 1)
        def _():
            prepare_b(c + 1)

        @pl.when(c > 0)
        def _():
            stage2_zonal(c - 1)

        @pl.when(c > 1)
        def _():
            stage3(c - 2)

        @pl.when(c < CHUNKS - 2)
        def _():
            send_pooled(c + 2)
            prepare_a(c + 2)

        attend(c, 1)
        stage1(c)

        @pl.when(c > 0)
        def _():
            stage2_side(c - 1)

        @pl.when(c > 1)
        def _():
            relay_grads(c - 2)

        @pl.when(c > 2)
        def _():
            stage4(c - 3)

    stage2_zonal(CHUNKS - 1)
    stage3(CHUNKS - 2)
    stage2_side(CHUNKS - 1)
    relay_grads(CHUNKS - 2)
    stage3(CHUNKS - 1)
    stage4(1)
    stage4(2)
    stage4(3)

    @pl.loop(0, CHUNKS)
    def _(c):
        below, above = lat_copies(c)
        to_up, to_down = grad_lat_copies(c)

        @pl.when(lat < lats - 1)
        def _():
            for copy in below + [to_down]:
                copy.wait_send()

        @pl.when(lat > 0)
        def _():
            for copy in above + [to_up]:
                copy.wait_send()

        for copy in edge_copies(c) + corner_copies(c) + side_copies(c) + [zonal_core(c), zonal_y(c), gather_c(c, core)]:
            copy.wait_send()
        for d in range(1, ZN):
            zonal_z(c, d).wait_send()
            gather_z(c, d).wait_send()

        @pl.when(crosses & (c > 0))
        def _():
            pass_on(c).wait_send()

        @pl.when(crosses & (c < CHUNKS - 1))
        def _():
            pass_on_grads(c).wait_send()

    gather_y(why).wait_send()


def body(queries, keys, values, cotangent, near_pattern, zonal_pattern):
    block = jax.ShapeDtypeStruct(queries.shape, BF)
    dma = pltpu.SemaphoreType.DMA
    vm = pltpu.VMEM
    scratch = [
        vm((CHUNKS, 2, TILES, 16, LANES), BF),
        vm((CHUNKS, 2, 2, 4, 16, LANES), BF),
        vm((CHUNKS, 2, 2, 2, 3, 16, LANES), BF),
        vm((CHUNKS, 2, 2, ZN, 16, LANES), BF),
        vm((8, 640, 256), F32),
        vm((SECT * 8, 128), F32),
        vm((32, 512), F32),
        vm((TILES * 16, 256), F32),
        vm((TILES * 16, 256), BF),
        vm((CHUNKS, 2, REGION, 16, LANES), F32),
        vm((CHUNKS, 2, 2, 10, 16, LANES), BF),
        vm((CHUNKS, 2, 2, 10, 16, LANES), BF),
        vm((CHUNKS, 2, 2, 6, 16, LANES), BF),
        vm((CHUNKS, 2, 2, 6, 16, LANES), BF),
        vm((CHUNKS, 2, 16, 16, LANES), BF),
        vm((CHUNKS, 16, 16, LANES), BF),
        vm((CHUNKS, 16, 16, LANES), BF),
        vm((CHUNKS, 8, 16, LANES), BF),
        vm((CHUNKS, 8, 16, LANES), BF),
        vm((CHUNKS, 8, 16, LANES), BF),
        vm((CHUNKS, 2, 6, 16, LANES), BF),
        vm((CHUNKS, 2, 6, 16, LANES), BF),
    ]
    sems = [(CHUNKS, 2), (CHUNKS,), (CHUNKS,), (CHUNKS,), (CHUNKS, 4), (CHUNKS, 2), (CHUNKS, 4), (CHUNKS, ZN), (1,), (CHUNKS,), (CHUNKS, 2), (CHUNKS, 2), (CHUNKS,), (CHUNKS,), (CHUNKS, ZN)]
    for shape in sems:
        scratch += [dma(shape), dma(shape)]
    return pl.pallas_call(
        kernel,
        out_shape=[block] * 4,
        in_specs=[pl.BlockSpec(memory_space=pltpu.VMEM)] * 6,
        out_specs=[pl.BlockSpec(memory_space=pltpu.VMEM)] * 4,
        scratch_shapes=scratch,
        compiler_params=pltpu.CompilerParams(
            collective_id=0, has_side_effects=True, vmem_limit_bytes=56 * 1024 * 1024
        ),
        cost_estimate=pl.CostEstimate(flops=3_000_000_000, bytes_accessed=2 << 20, transcendentals=1 << 20),
    )(queries, keys, values, cotangent, near_pattern, zonal_pattern)


def solution(mesh):
    grid = P("lat", "lon", None)
    return jax.shard_map(
        body,
        mesh=mesh,
        in_specs=(grid, grid, grid, grid, P(), P("lat", None)),
        out_specs=(grid, grid, grid, grid),
        check_vma=False,
    )
```

```python
import jax
import jax.numpy as jnp
from jax import lax
from jax.experimental import pallas as pl
from jax.experimental.pallas import tpu as pltpu
from jax.sharding import PartitionSpec as P

MESH = pl.DeviceIdType.MESH
RADIUS = 6
SPAN = 2 * RADIUS + 1
ROWS = 8
COLS = 16
REGION = ROWS + 2 * RADIUS
SECT = 32
ZN = 8
LANES = 256
CHUNKS = 4
TILES = 56
CENTRE, LEFT, RIGHT, ZONAL = 0, 20, 30, 40
NEVER = -1e30
BF, F32 = jnp.bfloat16, jnp.float32


def kernel(
    q_ref, k_ref, v_ref, do_ref, near_ref, zonal_ref,
    att_ref, gq_ref, gk_ref, gv_ref,
    kv, edge, corner, gath, bias, bias_z, wide, pattern, scores, probs, dscores,
    acc, side_out, side_in, lat_out, lat_in,
    z_out, z_in1, z_mid1, z_in2, z_mid2, z_in3,
    relay, relay_g, rel_s, rel_r, fwd_s, fwd_r, relg_s, relg_r, fwdg_s, fwdg_r,
    lat_s, lat_r, edge_s, edge_r, cor_s, cor_r,
    g_s, g_r, gy_s, gy_r, gc_s, gc_r,
    side_s, side_r, glat_s, glat_r, zc_s, zc_r, zy_s, zy_r, zz_s, zz_r,
):
    lat, lon = lax.axis_index("lat"), lax.axis_index("lon")
    lats, lons = lax.axis_size("lat"), lax.axis_size("lon")
    core, zed, why = lon % 2, (lon // 2) % ZN, lon // (2 * ZN)

    def lon_of(y, z, c):
        return (y * ZN + z) * 2 + c

    up, down = (lat + lats - 1) % lats, (lat + 1) % lats
    west, east = (lon + lons - 1) % lons, (lon + 1) % lons
    core_peer = lon_of(why, zed, 1 - core)
    y_peer = lon_of(1 - why, zed, core)
    z_peers = [None] + [lon_of(why, (zed + d) % ZN, core) for d in range(1, ZN)]

    barrier = pltpu.get_barrier_semaphore()
    greeted = [(up, lon), (down, lon), (lat, west), (lat, east), (lat, core_peer), (lat, y_peer)]
    greeted += [(lat, peer) for peer in z_peers[1:]]
    for peer in greeted:
        pl.semaphore_signal(barrier, inc=1, device_id=peer, device_id_type=MESH)

    middle = lats // 2
    crosses = (lat == middle - 1) | (lat == middle)
    far_down, far_up = lat == middle - 1, lat == middle

    @pl.when(far_down)
    def _():
        pl.semaphore_signal(barrier, inc=1, device_id=(down, y_peer), device_id_type=MESH)

    @pl.when(far_up)
    def _():
        pl.semaphore_signal(barrier, inc=1, device_id=(up, y_peer), device_id_type=MESH)

    def remote(src, dst, send, recv, peer):
        return pltpu.make_async_remote_copy(
            src_ref=src, dst_ref=dst, send_sem=send, recv_sem=recv, device_id=peer, device_id_type=MESH
        )

    def lanes(c):
        return pl.ds(pl.multiple_of(c * LANES, LANES), LANES)

    def lat_copies(c):
        below = [
            remote(ref.at[2:8, :, lanes(c)], kv.at[c, i, 0:6], lat_s.at[c, i], lat_r.at[c, i], (down, lon))
            for i, ref in enumerate((k_ref, v_ref))
        ]
        above = [
            remote(ref.at[0:6, :, lanes(c)], kv.at[c, i, 14:20], lat_s.at[c, 2 + i], lat_r.at[c, 2 + i], (up, lon))
            for i, ref in enumerate((k_ref, v_ref))
        ]
        return below, above

    def cross_copies(c):
        below = [
            remote(ref.at[2:8, :, lanes(c)], relay.at[c, i], lat_s.at[c, i], rel_r.at[c, i], (down, y_peer))
            for i, ref in enumerate((k_ref, v_ref))
        ]
        above = [
            remote(ref.at[0:6, :, lanes(c)], relay.at[c, i], lat_s.at[c, 2 + i], rel_r.at[c, i], (up, y_peer))
            for i, ref in enumerate((k_ref, v_ref))
        ]
        return below, above

    def pass_on(c):
        at = kv.at[c, :, pl.ds((middle - lat) * (REGION - 6), 6)]
        return remote(relay.at[c], at, fwd_s.at[c], fwd_r.at[c], (lat, y_peer))

    def cross_grads(c):
        return [
            remote(lat_out.at[c, 0], relay_g.at[c], glat_s.at[c, 0], relg_r.at[c], (up, y_peer)),
            remote(lat_out.at[c, 1], relay_g.at[c], glat_s.at[c, 1], relg_r.at[c], (down, y_peer)),
        ]

    def pass_on_grads(c):
        at = lat_in.at[c, lat - middle + 1]
        return remote(relay_g.at[c], at, fwdg_s.at[c], fwdg_r.at[c], (lat, y_peer))

    def edge_copies(c):
        return [
            remote(edge.at[c, 0], kv.at[c, :, LEFT + 3 : LEFT + 7], edge_s.at[c, 0], edge_r.at[c, 0], (lat, east)),
            remote(edge.at[c, 1], kv.at[c, :, RIGHT + 3 : RIGHT + 7], edge_s.at[c, 1], edge_r.at[c, 1], (lat, west)),
        ]

    def corner_copies(c):
        out = []
        for i, (base, peer) in enumerate(((LEFT, east), (RIGHT, west))):
            for j, first in enumerate((0, 7)):
                n = 2 * i + j
                out.append(
                    remote(
                        corner.at[c, i, j], kv.at[c, :, base + first : base + first + 3],
                        cor_s.at[c, n], cor_r.at[c, n], (lat, peer),
                    )
                )
        return out

    def gather_y(y):
        at = gath.at[:, core, y, zed]
        return remote(at, at, gy_s.at[0], gy_r.at[0], (lat, y_peer))

    def gather_z(c, d):
        at = gath.at[c, core, :, zed]
        return remote(at, at, g_s.at[c, d], g_r.at[c, d], (lat, z_peers[d]))

    def gather_z_wait(c, d):
        at = gath.at[c, core, :, (zed + ZN - d) % ZN]
        return remote(at, at, g_s.at[c, d], g_r.at[c, d], (lat, z_peers[d]))

    def gather_c(c, which):
        at = gath.at[c, which]
        return remote(at, at, gc_s.at[c], gc_r.at[c], (lat, core_peer))

    def side_copies(c):
        return [
            remote(side_out.at[c, 0], side_in.at[c, 0], side_s.at[c, 0], side_r.at[c, 0], (lat, west)),
            remote(side_out.at[c, 1], side_in.at[c, 1], side_s.at[c, 1], side_r.at[c, 1], (lat, east)),
        ]

    def grad_lat_copies(c):
        return [
            remote(lat_out.at[c, 0], lat_in.at[c, 0], glat_s.at[c, 0], glat_r.at[c, 0], (up, lon)),
            remote(lat_out.at[c, 1], lat_in.at[c, 1], glat_s.at[c, 1], glat_r.at[c, 1], (down, lon)),
        ]

    def zonal_core(c):
        return remote(z_out.at[c, 1 - core], z_in1.at[c], zc_s.at[c], zc_r.at[c], (lat, core_peer))

    def zonal_y(c):
        src = z_mid1.at[c, pl.ds((1 - why) * ZN, ZN)]
        return remote(src, z_in2.at[c], zy_s.at[c], zy_r.at[c], (lat, y_peer))

    def zonal_z(c, d):
        src = z_mid2.at[c, (zed + d) % ZN]
        return remote(src, z_in3.at[c, d], zz_s.at[c, d], zz_r.at[c, d], (lat, z_peers[d]))

    for i, ref in enumerate((k_ref, v_ref)):
        total = jnp.sum(ref[...].astype(F32), axis=1) * (COLS ** -0.5)
        if i == 0:
            pooled_keys = total
    pooled = jnp.concatenate([pooled_keys, total], axis=0).astype(BF)
    for c in range(CHUNKS):
        gath[c, core, why, zed] = pooled[:, c * LANES : (c + 1) * LANES]

    def pack_edges(c):
        for i, ref in enumerate((k_ref, v_ref)):
            block = ref[:, :, lanes(c)].astype(F32)
            edge[c, 0, i] = block[:, 8:16].reshape(64, LANES).astype(BF).reshape(4, 16, LANES)
            edge[c, 1, i] = block[:, 0:8].reshape(64, LANES).astype(BF).reshape(4, 16, LANES)

    @pl.loop(0, CHUNKS)
    def _(c):
        pack_edges(c)

    pl.semaphore_wait(barrier, len(greeted) + jnp.where(crosses, 1, 0))

    def send_rows(c):
        below, above = lat_copies(c)
        far_below, far_above = cross_copies(c)
        near = c == 0

        @pl.when((lat < lats - 1) & ((lat != middle - 1) | near))
        def _():
            for copy in below:
                copy.start()

        @pl.when(far_down & (not near))
        def _():
            for copy in far_below:
                copy.start()

        @pl.when((lat > 0) & ((lat != middle) | near))
        def _():
            for copy in above:
                copy.start()

        @pl.when(far_up & (not near))
        def _():
            for copy in far_above:
                copy.start()

    def send(c):
        for copy in edge_copies(c):
            copy.start()

    def send_pooled(c):
        for d in (4, 3, 5, 2, 6, 1, 7):
            gather_z(c, d).start()

    gather_y(why).start()
    send_rows(0)
    send(0)
    for c in range(1, CHUNKS):
        send_rows(c)

    @pl.loop(0, CHUNKS)
    def _(c):
        for i, ref in enumerate((k_ref, v_ref)):
            kv[c, i, 6:14] = ref[:, :, lanes(c)]

        @pl.when(lat == 0)
        def _():
            kv[c, :, 0:6] = jnp.zeros((2, 6, 16, LANES), BF)
            lat_in[c, 1] = jnp.zeros((2, 6, 16, LANES), BF)

        @pl.when(lat == lats - 1)
        def _():
            kv[c, :, 14:20] = jnp.zeros((2, 6, 16, LANES), BF)
            lat_in[c, 0] = jnp.zeros((2, 6, 16, LANES), BF)

    span_a = lax.broadcasted_iota(jnp.int32, (SPAN, 512), 0)
    lane_j = lax.broadcasted_iota(jnp.int32, (SPAN, 512), 1) // COLS
    select_a = ((REGION - 1 - lane_j) == span_a).astype(F32)
    centre = (lax.broadcasted_iota(jnp.int32, (SPAN, SPAN), 0) == RADIUS) & (
        lax.broadcasted_iota(jnp.int32, (SPAN, SPAN), 1) == RADIUS
    )
    sub = lax.broadcasted_iota(jnp.int32, (32, 512), 0)
    place = jnp.where(sub < 16, sub, jnp.where(sub < 24, sub - 24, sub - 8))
    offset = place - lax.broadcasted_iota(jnp.int32, (32, 512), 1) % COLS + RADIUS
    top_open = jnp.where(lat > 0, 0.0, NEVER).astype(F32)
    low_open = jnp.where(lat < lats - 1, 0.0, NEVER).astype(F32)

    def build_mask(pair):
        for half in range(2):
            head = pattern[pair * 2 + half]
            allowed = jnp.where((head == 1) | centre, 1.0, 0.0).astype(F32)
            by_lane = lax.dot_general(
                allowed, select_a, (((0,), (0,)), ((), ())), preferred_element_type=F32
            )
            full = jnp.full((32, 512), NEVER, F32)
            by_lane = (by_lane - 1.0) * (-NEVER)
            for b in range(SPAN):
                full = jnp.where(offset == b, by_lane[b : b + 1, :], full)
            wide[...] = full
            for row in range(REGION):
                start = (REGION - 1 - row) * COLS
                tile, phase = start // 128, start % 128
                if phase:
                    both = wide[:, tile * 128 : tile * 128 + 256]
                    part = pltpu.roll(both, 256 - phase, 1)[:, 0:128]
                else:
                    part = wide[:, tile * 128 : tile * 128 + 128]
                if row < RADIUS:
                    part = jnp.minimum(part, top_open)
                if row >= ROWS + RADIUS:
                    part = jnp.minimum(part, low_open)
                at = slice(half * 128, half * 128 + 128)
                bias[pair, row * 16 : row * 16 + 16, at] = part[0:16]
                bias[pair, 320 + row * 8 : 328 + row * 8, at] = part[16:24]
                bias[pair, 480 + row * 8 : 488 + row * 8, at] = part[24:32]

    row_of_lane = lax.broadcasted_iota(jnp.int32, (ROWS, 128), 1) // COLS
    row_hot = (row_of_lane == lax.broadcasted_iota(jnp.int32, (ROWS, 128), 0)).astype(F32)

    def build_zonal_mask():
        zonal_ok = jnp.where(zonal_ref[...] == 1, 1.0, 0.0).astype(F32)
        by_sector = lax.dot_general(zonal_ok, row_hot, (((0,), (0,)), ((), ())), preferred_element_type=F32)
        for n in range(SECT):
            s = n % 16 * 2 + n // 16
            bias_z[n * 8 : n * 8 + 8, :] = (by_sector[s : s + 1, :] * row_hot - 1.0) * (-NEVER)

    def relay_rows(c):
        @pl.when(crosses)
        def _():
            for copy in cross_copies(c)[0]:
                copy.wait_recv()
            pass_on(c).start()

    def prepare_a(c):
        below, above = lat_copies(c)
        near = c == 0

        @pl.when((lat > 0) & ((lat != middle) | near))
        def _():
            for copy in below:
                copy.wait_recv()

        @pl.when((lat < lats - 1) & ((lat != middle - 1) | near))
        def _():
            for copy in above:
                copy.wait_recv()

        @pl.when(crosses & jnp.logical_not(near))
        def _():
            pass_on(c).wait_recv()

        for i in range(2):
            for j, first in enumerate((0, 14)):
                block = kv[c, i, first : first + 6].astype(F32)
                corner[c, 0, j, i] = block[:, 8:16].reshape(48, LANES).astype(BF).reshape(3, 16, LANES)
                corner[c, 1, j, i] = block[:, 0:8].reshape(48, LANES).astype(BF).reshape(3, 16, LANES)
        for copy in corner_copies(c):
            copy.start()

    def prepare_b(c):
        for d in range(1, ZN):
            gather_z_wait(c, d).wait_recv()
        gather_c(c, core).start()

    for a in range(SPAN):
        pattern[:, a, :] = near_ref[a]

    def build_masks(first, last):
        @pl.loop(first, last)
        def _(pair):
            build_mask(pair)

    build_masks(0, 4)
    gather_y(1 - why).wait_recv()
    send_pooled(0)
    send(1)
    build_zonal_mask()
    build_masks(4, 8)
    prepare_a(0)
    send_pooled(1)
    send(2)
    relay_rows(1)
    prepare_b(0)
    relay_rows(2)
    send(3)
    prepare_a(1)

    low_half = lax.broadcasted_iota(jnp.int32, (128, 128), 1) < 64

    def split_pair(block):
        zero = jnp.zeros_like(block)
        both = jnp.concatenate([jnp.where(low_half, block, zero), jnp.where(low_half, zero, block)], axis=0)
        return both.astype(BF)

    def own_heads(product):
        return jnp.concatenate([product[0:64, 0:128], product[64:128, 128:256]], axis=0)

    NT = (((1,), (1,)), ((), ()))
    NN = (((1,), (0,)), ((), ()))
    TN = (((0,), (0,)), ((), ()))
    STEPS = TILES // 8

    def attend(c, half):
        here = slice(half * 128, half * 128 + 128)
        there = pl.ds(pl.multiple_of(c * LANES + half * 128, 128), 128)
        pair = c * 2 + half
        q_both = split_pair(q_ref[:, :, there].reshape(128, 128).astype(F32) * 0.125)
        grad = do_ref[:, :, there].reshape(128, 128).astype(F32)
        grad_both = split_pair(grad)
        kept = dict(highest=jnp.full((8, 256), NEVER, F32), total=jnp.zeros((8, 256), F32))

        def tokens(i, t):
            return kv[c, i, t * 8 : t * 8 + 8, :, here].reshape(128, 128)

        def all_tokens(i):
            return kv[c, i, :, :, here].reshape(TILES * 16, 128)

        def at(t):
            return slice(t * 128, t * 128 + 128)

        def score(t):
            s = lax.dot_general(tokens(0, t), q_both, NT, preferred_element_type=F32)
            if t < 5:
                s = s + bias[pair, at(t), :]
            else:
                z = bias_z[(t - 5) * 128 : (t - 4) * 128, :]
                s = s + jnp.concatenate([z, z], axis=1)
            scores[half, at(t), :] = s
            kept["highest"] = jnp.maximum(kept["highest"], jnp.max(s.reshape(16, 8, 256), axis=0))

        def exponential(t):
            if t == 0:
                kept["top"] = jnp.max(kept["highest"], axis=0, keepdims=True)
            e = jnp.exp(scores[half, at(t), :] - kept["top"])
            scores[half, at(t), :] = e
            kept["total"] = kept["total"] + jnp.sum(e.reshape(16, 8, 256), axis=0)

        def weigh(t):
            if t == 0:
                kept["inverse"] = 1.0 / jnp.sum(kept["total"], axis=0, keepdims=True)
            p = scores[half, at(t), :] * kept["inverse"]
            scores[half, at(t), :] = p
            probs[half, at(t), :] = p.astype(BF)

        def attended():
            out = lax.dot_general(all_tokens(1), probs[half], TN, preferred_element_type=F32)
            out = own_heads(out)
            att_ref[:, :, there] = out.T.astype(BF).reshape(8, 16, 128)
            prod = out * grad.T
            kept["delta"] = jnp.concatenate(
                [jnp.sum(prod[0:64], axis=0, keepdims=True), jnp.sum(prod[64:128], axis=0, keepdims=True)], axis=1
            )

        def back(t):
            dp = lax.dot_general(tokens(1, t), grad_both, NT, preferred_element_type=F32)
            ds = (scores[half, at(t), :] * (dp - kept["delta"])).astype(BF)
            dscores[half, at(t), :] = ds
            dk = lax.dot_general(ds, q_both, NN, preferred_element_type=F32)
            dv = lax.dot_general(probs[half, at(t), :], grad_both, NN, preferred_element_type=F32)
            if t < 5:
                for i, d in enumerate((dk, dv)):
                    d = d.reshape(8, 16, 128)
                    for n, (lo, hi) in enumerate(((CENTRE, LEFT), (LEFT, RIGHT), (RIGHT, ZONAL))):
                        first, last = max(lo, t * 8), min(hi, t * 8 + 8)
                        if first >= last:
                            continue
                        piece = d[first - t * 8 : last - t * 8]
                        if n == 0:
                            acc[c, i, first:last, :, here] = piece
                        else:
                            side_out[c, n - 1, i, first - lo : last - lo, :, here] = piece.astype(BF)
            else:
                both = jnp.concatenate([dk.reshape(16, 8, 128), dv.reshape(16, 8, 128)], axis=1)
                z_out[c, t - 5, :, :, here] = both.astype(BF)

        def query_grads():
            grad_q = lax.dot_general(all_tokens(0), dscores[half], TN, preferred_element_type=F32)
            grad_q = own_heads(grad_q) * 0.125
            gq_ref[:, :, there] = grad_q.T.astype(BF).reshape(8, 16, 128)

        passes = [score, exponential, weigh, back]
        steps = [[lambda t=t, f=f: f(t) for t in range(STEPS)] for f in passes]
        steps[2].append(attended)
        steps[3].append(query_grads)
        return steps

    def run(*lists):
        for n in range(max(len(steps) for steps in lists)):
            for steps in lists:
                if n < len(steps):
                    steps[n]()

    def attend_one(c, half):
        for steps in attend(c, half):
            run(steps)

    def attend_both(c):
        one, two = attend(c, 0), attend(c, 1)
        run(one[0])
        run(one[1], two[0])
        run(one[2], two[1])
        run(one[3], two[2])
        run(two[3])

    def load(c):
        gather_c(c, 1 - core).wait_recv()
        for first in range(2):
            block = gath[c, first].reshape(16, 16, LANES).astype(F32)
            for i in range(2):
                rows = block[:, i * 8 : i * 8 + 8].reshape(128, LANES).astype(BF)
                kv[c, i, ZONAL + first * 8 : ZONAL + first * 8 + 8] = rows.reshape(8, 16, LANES)
        for copy in edge_copies(c) + corner_copies(c):
            copy.wait_recv()

    def stage1(c):
        zonal_core(c).start()
        for copy in side_copies(c):
            copy.start()

    def stage2_zonal(c):
        zonal_core(c).wait_recv()
        z_mid1[c] = (z_out[c, core].astype(F32) + z_in1[c].astype(F32)).astype(BF)
        zonal_y(c).start()

    def stage2_side(c):
        for copy in side_copies(c):
            copy.wait_recv()
        for i in range(2):
            from_east = side_in[c, 0, i].astype(F32).reshape(REGION, 8, LANES)
            from_west = side_in[c, 1, i].astype(F32).reshape(REGION, 8, LANES)
            total = acc[c, i] + jnp.concatenate([from_west, from_east], axis=1)
            acc[c, i, 6:14] = total[6:14]
            lat_out[c, 0, i] = total[0:6].astype(BF)
            lat_out[c, 1, i] = total[14:20].astype(BF)
        to_up, to_down = grad_lat_copies(c)
        far_to_up, far_to_down = cross_grads(c)
        near = c == CHUNKS - 1

        @pl.when((lat > 0) & ((lat != middle) | near))
        def _():
            to_up.start()

        @pl.when(far_up & jnp.logical_not(near))
        def _():
            far_to_up.start()

        @pl.when((lat < lats - 1) & ((lat != middle - 1) | near))
        def _():
            to_down.start()

        @pl.when(far_down & jnp.logical_not(near))
        def _():
            far_to_down.start()

    def relay_grads(c):
        @pl.when(crosses)
        def _():
            cross_grads(c)[0].wait_recv()
            pass_on_grads(c).start()

    def stage3(c):
        zonal_y(c).wait_recv()
        z_mid2[c] = (z_mid1[c, pl.ds(why * ZN, ZN)].astype(F32) + z_in2[c].astype(F32)).astype(BF)
        for d in (4, 3, 5, 2, 6, 1, 7):
            zonal_z(c, d).start()

    def stage4(c):
        total = z_mid2[c, zed].astype(F32)
        for d in (1, 7, 2, 6, 3, 5, 4):
            zonal_z(c, d).wait_recv()
            total = total + z_in3[c, d].astype(F32)
        total = total * (COLS ** -0.5)
        to_up, to_down = grad_lat_copies(c)
        near = c == CHUNKS - 1

        @pl.when((lat < lats - 1) & ((lat != middle - 1) | near))
        def _():
            to_up.wait_recv()

        @pl.when((lat > 0) & ((lat != middle) | near))
        def _():
            to_down.wait_recv()

        @pl.when(crosses & jnp.logical_not(near))
        def _():
            pass_on_grads(c).wait_recv()

        for i, ref in enumerate((gk_ref, gv_ref)):
            for r in range(ROWS):
                row = acc[c, i, 6 + r] + total[i * 8 + r : i * 8 + r + 1, :]
                if r >= 2:
                    row = row + lat_in[c, 0, i, r - 2].astype(F32)
                if r < 6:
                    row = row + lat_in[c, 1, i, r].astype(F32)
                ref[r, :, lanes(c)] = row.astype(BF)

    @pl.loop(0, CHUNKS)
    def _(c):
        load(c)

        @pl.when(c == 0)
        def _():
            relay_rows(3)

        @pl.when(c < CHUNKS - 1)
        def _():
            prepare_b(c + 1)

        @pl.when(c < CHUNKS - 2)
        def _():
            send_pooled(c + 2)

        attend_both(c)
        stage1(c)

        @pl.when(c < CHUNKS - 2)
        def _():
            prepare_a(c + 2)

        @pl.when(c > 0)
        def _():
            stage2_zonal(c - 1)

        @pl.when(c > 1)
        def _():
            stage3(c - 2)

        @pl.when((c > 0) & (c < CHUNKS - 1))
        def _():
            stage2_side(c - 1)

    stage2_zonal(CHUNKS - 1)
    stage2_side(CHUNKS - 2)
    relay_grads(0)
    relay_grads(1)
    stage3(CHUNKS - 2)
    stage3(CHUNKS - 1)
    stage2_side(CHUNKS - 1)
    stage4(0)
    relay_grads(2)
    stage4(1)
    stage4(2)
    stage4(3)

    @pl.loop(0, CHUNKS)
    def _(c):
        below, above = lat_copies(c)
        to_up, to_down = grad_lat_copies(c)

        @pl.when(lat < lats - 1)
        def _():
            for copy in below + [to_down]:
                copy.wait_send()

        @pl.when(lat > 0)
        def _():
            for copy in above + [to_up]:
                copy.wait_send()

        for copy in edge_copies(c) + corner_copies(c) + side_copies(c) + [zonal_core(c), zonal_y(c), gather_c(c, core)]:
            copy.wait_send()
        for d in range(1, ZN):
            zonal_z(c, d).wait_send()
            gather_z(c, d).wait_send()

        @pl.when(crosses & (c > 0))
        def _():
            pass_on(c).wait_send()

        @pl.when(crosses & (c < CHUNKS - 1))
        def _():
            pass_on_grads(c).wait_send()

    gather_y(why).wait_send()


def hand_over(*refs):
    for src, dst in zip(refs[:4], refs[4:]):
        dst[...] = src[...]


def body(queries, keys, values, cotangent, near_pattern, zonal_pattern):
    block = jax.ShapeDtypeStruct(queries.shape, BF)
    dma = pltpu.SemaphoreType.DMA
    vm = pltpu.VMEM
    scratch = [
        vm((CHUNKS, 2, TILES, 16, LANES), BF),
        vm((CHUNKS, 2, 2, 4, 16, LANES), BF),
        vm((CHUNKS, 2, 2, 2, 3, 16, LANES), BF),
        vm((CHUNKS, 2, 2, ZN, 16, LANES), BF),
        vm((8, 640, 256), F32),
        vm((SECT * 8, 128), F32),
        vm((32, 512), F32),
        vm((16, SPAN, SPAN), jnp.int32),
        vm((2, TILES * 16, 256), F32),
        vm((2, TILES * 16, 256), BF),
        vm((2, TILES * 16, 256), BF),
        vm((CHUNKS, 2, REGION, 16, LANES), F32),
        vm((CHUNKS, 2, 2, 10, 16, LANES), BF),
        vm((CHUNKS, 2, 2, 10, 16, LANES), BF),
        vm((CHUNKS, 2, 2, 6, 16, LANES), BF),
        vm((CHUNKS, 2, 2, 6, 16, LANES), BF),
        vm((CHUNKS, 2, 16, 16, LANES), BF),
        vm((CHUNKS, 16, 16, LANES), BF),
        vm((CHUNKS, 16, 16, LANES), BF),
        vm((CHUNKS, 8, 16, LANES), BF),
        vm((CHUNKS, 8, 16, LANES), BF),
        vm((CHUNKS, 8, 16, LANES), BF),
        vm((CHUNKS, 2, 6, 16, LANES), BF),
        vm((CHUNKS, 2, 6, 16, LANES), BF),
    ]
    sems = [(CHUNKS, 2), (CHUNKS,), (CHUNKS,), (CHUNKS,), (CHUNKS, 4), (CHUNKS, 2), (CHUNKS, 4), (CHUNKS, ZN), (1,), (CHUNKS,), (CHUNKS, 2), (CHUNKS, 2), (CHUNKS,), (CHUNKS,), (CHUNKS, ZN)]
    for shape in sems:
        scratch += [dma(shape), dma(shape)]
    results = pl.pallas_call(
        kernel,
        out_shape=[block] * 4,
        in_specs=[pl.BlockSpec(memory_space=pltpu.VMEM)] * 6,
        out_specs=[pl.BlockSpec(memory_space=pltpu.VMEM)] * 4,
        scratch_shapes=scratch,
        compiler_params=pltpu.CompilerParams(
            collective_id=0, has_side_effects=True, vmem_limit_bytes=56 * 1024 * 1024
        ),
        cost_estimate=pl.CostEstimate(flops=3_000_000_000, bytes_accessed=2 << 20, transcendentals=1 << 20),
    )(queries, keys, values, cotangent, jnp.swapaxes(near_pattern, 0, 1), zonal_pattern)

    return pl.pallas_call(
        hand_over,
        out_shape=[block] * 4,
        in_specs=[pl.BlockSpec(memory_space=pltpu.VMEM)] * 4,
        out_specs=[pl.BlockSpec(memory_space=pltpu.VMEM)] * 4,
    )(*results)


def solution(mesh):
    grid = P("lat", "lon", None)
    return jax.shard_map(
        body,
        mesh=mesh,
        in_specs=(grid, grid, grid, grid, P(), P("lat", None)),
        out_specs=(grid, grid, grid, grid),
        check_vma=False,
    )
```

```python
import jax
import jax.numpy as jnp
from jax import lax
from jax.experimental import pallas as pl
from jax.experimental.pallas import tpu as pltpu
from jax.sharding import PartitionSpec as P

MESH = pl.DeviceIdType.MESH
RADIUS = 6
SPAN = 2 * RADIUS + 1
ROWS = 8
COLS = 16
REGION = ROWS + 2 * RADIUS
SECT = 32
ZN = 8
LANES = 256
CHUNKS = 4
TILES = 56
CENTRE, LEFT, RIGHT, ZONAL = 0, 20, 30, 40
NEVER = -1e30
BF, F32 = jnp.bfloat16, jnp.float32


def kernel(
    q_in, k_in, v_in, do_in, near_ref, zonal_ref,
    att_out, gq_out, gk_ref, gv_ref,
    q_ref, k_ref, v_ref, do_ref, att_ref, gq_ref, in_sem, out_sem,
    kv, edge, corner, gath, bias, bias_z, wide, pattern, scores, probs, dscores,
    acc, side_out, side_in, lat_out, lat_in,
    z_out, z_in1, z_mid1, z_in2, z_mid2, z_in3,
    relay, relay_g, rel_s, rel_r, fwd_s, fwd_r, relg_s, relg_r, fwdg_s, fwdg_r,
    lat_s, lat_r, edge_s, edge_r, cor_s, cor_r,
    g_s, g_r, gy_s, gy_r, gc_s, gc_r,
    side_s, side_r, glat_s, glat_r, zc_s, zc_r, zy_s, zy_r, zz_s, zz_r,
):
    lat, lon = lax.axis_index("lat"), lax.axis_index("lon")
    lats, lons = lax.axis_size("lat"), lax.axis_size("lon")
    core, zed, why = lon % 2, (lon // 2) % ZN, lon // (2 * ZN)

    def lon_of(y, z, c):
        return (y * ZN + z) * 2 + c

    up, down = (lat + lats - 1) % lats, (lat + 1) % lats
    west, east = (lon + lons - 1) % lons, (lon + 1) % lons
    core_peer = lon_of(why, zed, 1 - core)
    y_peer = lon_of(1 - why, zed, core)
    z_peers = [None] + [lon_of(why, (zed + d) % ZN, core) for d in range(1, ZN)]

    barrier = pltpu.get_barrier_semaphore()
    greeted = [(up, lon), (down, lon), (lat, west), (lat, east), (lat, core_peer), (lat, y_peer)]
    greeted += [(lat, peer) for peer in z_peers[1:]]
    for peer in greeted:
        pl.semaphore_signal(barrier, inc=1, device_id=peer, device_id_type=MESH)

    middle = lats // 2
    crosses = (lat == middle - 1) | (lat == middle)
    far_down, far_up = lat == middle - 1, lat == middle

    @pl.when(far_down)
    def _():
        pl.semaphore_signal(barrier, inc=1, device_id=(down, y_peer), device_id_type=MESH)

    @pl.when(far_up)
    def _():
        pl.semaphore_signal(barrier, inc=1, device_id=(up, y_peer), device_id_type=MESH)

    loads = [
        pltpu.make_async_copy(src, dst, in_sem.at[n])
        for n, (src, dst) in enumerate(((k_in, k_ref), (v_in, v_ref), (q_in, q_ref), (do_in, do_ref)))
    ]
    for load_one in loads:
        load_one.start()
    for load_one in loads:
        load_one.wait()
    stores = [
        pltpu.make_async_copy(src, dst, out_sem.at[n])
        for n, (src, dst) in enumerate(((att_ref, att_out), (gq_ref, gq_out)))
    ]

    def remote(src, dst, send, recv, peer):
        return pltpu.make_async_remote_copy(
            src_ref=src, dst_ref=dst, send_sem=send, recv_sem=recv, device_id=peer, device_id_type=MESH
        )

    def lanes(c):
        return pl.ds(pl.multiple_of(c * LANES, LANES), LANES)

    def lat_copies(c):
        below = [
            remote(ref.at[2:8, :, lanes(c)], kv.at[c, i, 0:6], lat_s.at[c, i], lat_r.at[c, i], (down, lon))
            for i, ref in enumerate((k_ref, v_ref))
        ]
        above = [
            remote(ref.at[0:6, :, lanes(c)], kv.at[c, i, 14:20], lat_s.at[c, 2 + i], lat_r.at[c, 2 + i], (up, lon))
            for i, ref in enumerate((k_ref, v_ref))
        ]
        return below, above

    def cross_copies(c):
        below = [
            remote(ref.at[2:8, :, lanes(c)], relay.at[c, i], lat_s.at[c, i], rel_r.at[c, i], (down, y_peer))
            for i, ref in enumerate((k_ref, v_ref))
        ]
        above = [
            remote(ref.at[0:6, :, lanes(c)], relay.at[c, i], lat_s.at[c, 2 + i], rel_r.at[c, i], (up, y_peer))
            for i, ref in enumerate((k_ref, v_ref))
        ]
        return below, above

    def pass_on(c):
        at = kv.at[c, :, pl.ds((middle - lat) * (REGION - 6), 6)]
        return remote(relay.at[c], at, fwd_s.at[c], fwd_r.at[c], (lat, y_peer))

    def cross_grads(c):
        return [
            remote(lat_out.at[c, 0], relay_g.at[c], glat_s.at[c, 0], relg_r.at[c], (up, y_peer)),
            remote(lat_out.at[c, 1], relay_g.at[c], glat_s.at[c, 1], relg_r.at[c], (down, y_peer)),
        ]

    def pass_on_grads(c):
        at = lat_in.at[c, lat - middle + 1]
        return remote(relay_g.at[c], at, fwdg_s.at[c], fwdg_r.at[c], (lat, y_peer))

    def edge_copies(c):
        return [
            remote(edge.at[c, 0], kv.at[c, :, LEFT + 3 : LEFT + 7], edge_s.at[c, 0], edge_r.at[c, 0], (lat, east)),
            remote(edge.at[c, 1], kv.at[c, :, RIGHT + 3 : RIGHT + 7], edge_s.at[c, 1], edge_r.at[c, 1], (lat, west)),
        ]

    def corner_copies(c):
        out = []
        for i, (base, peer) in enumerate(((LEFT, east), (RIGHT, west))):
            for j, first in enumerate((0, 7)):
                n = 2 * i + j
                out.append(
                    remote(
                        corner.at[c, i, j], kv.at[c, :, base + first : base + first + 3],
                        cor_s.at[c, n], cor_r.at[c, n], (lat, peer),
                    )
                )
        return out

    def gather_y(y):
        at = gath.at[:, core, y, zed]
        return remote(at, at, gy_s.at[0], gy_r.at[0], (lat, y_peer))

    def gather_z(c, d):
        at = gath.at[c, core, :, zed]
        return remote(at, at, g_s.at[c, d], g_r.at[c, d], (lat, z_peers[d]))

    def gather_z_wait(c, d):
        at = gath.at[c, core, :, (zed + ZN - d) % ZN]
        return remote(at, at, g_s.at[c, d], g_r.at[c, d], (lat, z_peers[d]))

    def gather_c(c, which):
        at = gath.at[c, which]
        return remote(at, at, gc_s.at[c], gc_r.at[c], (lat, core_peer))

    def side_copies(c):
        return [
            remote(side_out.at[c, 0], side_in.at[c, 0], side_s.at[c, 0], side_r.at[c, 0], (lat, west)),
            remote(side_out.at[c, 1], side_in.at[c, 1], side_s.at[c, 1], side_r.at[c, 1], (lat, east)),
        ]

    def grad_lat_copies(c):
        return [
            remote(lat_out.at[c, 0], lat_in.at[c, 0], glat_s.at[c, 0], glat_r.at[c, 0], (up, lon)),
            remote(lat_out.at[c, 1], lat_in.at[c, 1], glat_s.at[c, 1], glat_r.at[c, 1], (down, lon)),
        ]

    def zonal_core(c):
        return remote(z_out.at[c, 1 - core], z_in1.at[c], zc_s.at[c], zc_r.at[c], (lat, core_peer))

    def zonal_y(c):
        src = z_mid1.at[c, pl.ds((1 - why) * ZN, ZN)]
        return remote(src, z_in2.at[c], zy_s.at[c], zy_r.at[c], (lat, y_peer))

    def zonal_z(c, d):
        src = z_mid2.at[c, (zed + d) % ZN]
        return remote(src, z_in3.at[c, d], zz_s.at[c, d], zz_r.at[c, d], (lat, z_peers[d]))

    for i, ref in enumerate((k_ref, v_ref)):
        total = jnp.sum(ref[...].astype(F32), axis=1) * (COLS ** -0.5)
        if i == 0:
            pooled_keys = total
    pooled = jnp.concatenate([pooled_keys, total], axis=0).astype(BF)
    for c in range(CHUNKS):
        gath[c, core, why, zed] = pooled[:, c * LANES : (c + 1) * LANES]

    def pack_edges(c):
        for i, ref in enumerate((k_ref, v_ref)):
            block = ref[:, :, lanes(c)].astype(F32)
            edge[c, 0, i] = block[:, 8:16].reshape(64, LANES).astype(BF).reshape(4, 16, LANES)
            edge[c, 1, i] = block[:, 0:8].reshape(64, LANES).astype(BF).reshape(4, 16, LANES)

    @pl.loop(0, CHUNKS)
    def _(c):
        pack_edges(c)

    pl.semaphore_wait(barrier, len(greeted) + jnp.where(crosses, 1, 0))

    def send_rows(c):
        below, above = lat_copies(c)
        far_below, far_above = cross_copies(c)
        near = c == 0

        @pl.when((lat < lats - 1) & ((lat != middle - 1) | near))
        def _():
            for copy in below:
                copy.start()

        @pl.when(far_down & (not near))
        def _():
            for copy in far_below:
                copy.start()

        @pl.when((lat > 0) & ((lat != middle) | near))
        def _():
            for copy in above:
                copy.start()

        @pl.when(far_up & (not near))
        def _():
            for copy in far_above:
                copy.start()

    def send(c):
        for copy in edge_copies(c):
            copy.start()

    def send_pooled(c):
        for d in (4, 3, 5, 2, 6, 1, 7):
            gather_z(c, d).start()

    gather_y(why).start()
    send_rows(0)
    send(0)
    for c in range(1, CHUNKS):
        send_rows(c)

    @pl.loop(0, CHUNKS)
    def _(c):
        for i, ref in enumerate((k_ref, v_ref)):
            kv[c, i, 6:14] = ref[:, :, lanes(c)]

        @pl.when(lat == 0)
        def _():
            kv[c, :, 0:6] = jnp.zeros((2, 6, 16, LANES), BF)
            lat_in[c, 1] = jnp.zeros((2, 6, 16, LANES), BF)

        @pl.when(lat == lats - 1)
        def _():
            kv[c, :, 14:20] = jnp.zeros((2, 6, 16, LANES), BF)
            lat_in[c, 0] = jnp.zeros((2, 6, 16, LANES), BF)

    span_a = lax.broadcasted_iota(jnp.int32, (SPAN, 512), 0)
    lane_j = lax.broadcasted_iota(jnp.int32, (SPAN, 512), 1) // COLS
    select_a = ((REGION - 1 - lane_j) == span_a).astype(F32)
    centre = (lax.broadcasted_iota(jnp.int32, (SPAN, SPAN), 0) == RADIUS) & (
        lax.broadcasted_iota(jnp.int32, (SPAN, SPAN), 1) == RADIUS
    )
    sub = lax.broadcasted_iota(jnp.int32, (32, 512), 0)
    place = jnp.where(sub < 16, sub, jnp.where(sub < 24, sub - 24, sub - 8))
    offset = place - lax.broadcasted_iota(jnp.int32, (32, 512), 1) % COLS + RADIUS
    top_open = jnp.where(lat > 0, 0.0, NEVER).astype(F32)
    low_open = jnp.where(lat < lats - 1, 0.0, NEVER).astype(F32)

    def build_mask(pair):
        for half in range(2):
            head = pattern[pair * 2 + half]
            allowed = jnp.where((head == 1) | centre, 1.0, 0.0).astype(F32)
            by_lane = lax.dot_general(
                allowed, select_a, (((0,), (0,)), ((), ())), preferred_element_type=F32
            )
            full = jnp.full((32, 512), NEVER, F32)
            by_lane = (by_lane - 1.0) * (-NEVER)
            for b in range(SPAN):
                full = jnp.where(offset == b, by_lane[b : b + 1, :], full)
            wide[...] = full
            for row in range(REGION):
                start = (REGION - 1 - row) * COLS
                tile, phase = start // 128, start % 128
                if phase:
                    both = wide[:, tile * 128 : tile * 128 + 256]
                    part = pltpu.roll(both, 256 - phase, 1)[:, 0:128]
                else:
                    part = wide[:, tile * 128 : tile * 128 + 128]
                if row < RADIUS:
                    part = jnp.minimum(part, top_open)
                if row >= ROWS + RADIUS:
                    part = jnp.minimum(part, low_open)
                at = slice(half * 128, half * 128 + 128)
                bias[pair, row * 16 : row * 16 + 16, at] = part[0:16]
                bias[pair, 320 + row * 8 : 328 + row * 8, at] = part[16:24]
                bias[pair, 480 + row * 8 : 488 + row * 8, at] = part[24:32]

    row_of_lane = lax.broadcasted_iota(jnp.int32, (ROWS, 128), 1) // COLS
    row_hot = (row_of_lane == lax.broadcasted_iota(jnp.int32, (ROWS, 128), 0)).astype(F32)

    def build_zonal_mask():
        zonal_ok = jnp.where(zonal_ref[...] == 1, 1.0, 0.0).astype(F32)
        by_sector = lax.dot_general(zonal_ok, row_hot, (((0,), (0,)), ((), ())), preferred_element_type=F32)
        for n in range(SECT):
            s = n % 16 * 2 + n // 16
            bias_z[n * 8 : n * 8 + 8, :] = (by_sector[s : s + 1, :] * row_hot - 1.0) * (-NEVER)

    def relay_rows(c):
        @pl.when(crosses)
        def _():
            for copy in cross_copies(c)[0]:
                copy.wait_recv()
            pass_on(c).start()

    def prepare_a(c):
        below, above = lat_copies(c)
        near = c == 0

        @pl.when((lat > 0) & ((lat != middle) | near))
        def _():
            for copy in below:
                copy.wait_recv()

        @pl.when((lat < lats - 1) & ((lat != middle - 1) | near))
        def _():
            for copy in above:
                copy.wait_recv()

        @pl.when(crosses & jnp.logical_not(near))
        def _():
            pass_on(c).wait_recv()

        for i in range(2):
            for j, first in enumerate((0, 14)):
                block = kv[c, i, first : first + 6].astype(F32)
                corner[c, 0, j, i] = block[:, 8:16].reshape(48, LANES).astype(BF).reshape(3, 16, LANES)
                corner[c, 1, j, i] = block[:, 0:8].reshape(48, LANES).astype(BF).reshape(3, 16, LANES)
        for copy in corner_copies(c):
            copy.start()

    def prepare_b(c):
        for d in range(1, ZN):
            gather_z_wait(c, d).wait_recv()
        gather_c(c, core).start()

    for a in range(SPAN):
        pattern[:, a, :] = near_ref[a]

    def build_masks(first, last):
        @pl.loop(first, last)
        def _(pair):
            build_mask(pair)

    build_masks(0, 4)
    gather_y(1 - why).wait_recv()
    send_pooled(0)
    send(1)
    build_zonal_mask()
    build_masks(4, 8)
    prepare_a(0)
    send_pooled(1)
    send(2)
    relay_rows(1)
    prepare_b(0)
    relay_rows(2)
    send(3)
    prepare_a(1)

    low_half = lax.broadcasted_iota(jnp.int32, (128, 128), 1) < 64

    def split_pair(block):
        zero = jnp.zeros_like(block)
        both = jnp.concatenate([jnp.where(low_half, block, zero), jnp.where(low_half, zero, block)], axis=0)
        return both.astype(BF)

    def own_heads(product):
        return jnp.concatenate([product[0:64, 0:128], product[64:128, 128:256]], axis=0)

    NT = (((1,), (1,)), ((), ()))
    NN = (((1,), (0,)), ((), ()))
    TN = (((0,), (0,)), ((), ()))
    STEPS = TILES // 8

    def attend(c, half):
        here = slice(half * 128, half * 128 + 128)
        there = pl.ds(pl.multiple_of(c * LANES + half * 128, 128), 128)
        pair = c * 2 + half
        q_both = split_pair(q_ref[:, :, there].reshape(128, 128).astype(F32) * 0.125)
        grad = do_ref[:, :, there].reshape(128, 128).astype(F32)
        grad_both = split_pair(grad)
        kept = dict(highest=jnp.full((8, 256), NEVER, F32), total=jnp.zeros((8, 256), F32))

        def tokens(i, t):
            return kv[c, i, t * 8 : t * 8 + 8, :, here].reshape(128, 128)

        def all_tokens(i):
            return kv[c, i, :, :, here].reshape(TILES * 16, 128)

        def at(t):
            return slice(t * 128, t * 128 + 128)

        def score(t):
            s = lax.dot_general(tokens(0, t), q_both, NT, preferred_element_type=F32)
            if t < 5:
                s = s + bias[pair, at(t), :]
            else:
                z = bias_z[(t - 5) * 128 : (t - 4) * 128, :]
                s = s + jnp.concatenate([z, z], axis=1)
            scores[half, at(t), :] = s
            kept["highest"] = jnp.maximum(kept["highest"], jnp.max(s.reshape(16, 8, 256), axis=0))

        def exponential(t):
            if t == 0:
                kept["top"] = jnp.max(kept["highest"], axis=0, keepdims=True)
            e = jnp.exp(scores[half, at(t), :] - kept["top"])
            scores[half, at(t), :] = e
            kept["total"] = kept["total"] + jnp.sum(e.reshape(16, 8, 256), axis=0)

        def weigh(t):
            if t == 0:
                kept["inverse"] = 1.0 / jnp.sum(kept["total"], axis=0, keepdims=True)
            p = scores[half, at(t), :] * kept["inverse"]
            scores[half, at(t), :] = p
            probs[half, at(t), :] = p.astype(BF)

        def attended():
            out = lax.dot_general(all_tokens(1), probs[half], TN, preferred_element_type=F32)
            out = own_heads(out)
            att_ref[:, :, there] = out.T.astype(BF).reshape(8, 16, 128)
            prod = out * grad.T
            kept["delta"] = jnp.concatenate(
                [jnp.sum(prod[0:64], axis=0, keepdims=True), jnp.sum(prod[64:128], axis=0, keepdims=True)], axis=1
            )

        def back(t):
            dp = lax.dot_general(tokens(1, t), grad_both, NT, preferred_element_type=F32)
            ds = (scores[half, at(t), :] * (dp - kept["delta"])).astype(BF)
            dscores[half, at(t), :] = ds
            dk = lax.dot_general(ds, q_both, NN, preferred_element_type=F32)
            dv = lax.dot_general(probs[half, at(t), :], grad_both, NN, preferred_element_type=F32)
            if t < 5:
                for i, d in enumerate((dk, dv)):
                    d = d.reshape(8, 16, 128)
                    for n, (lo, hi) in enumerate(((CENTRE, LEFT), (LEFT, RIGHT), (RIGHT, ZONAL))):
                        first, last = max(lo, t * 8), min(hi, t * 8 + 8)
                        if first >= last:
                            continue
                        piece = d[first - t * 8 : last - t * 8]
                        if n == 0:
                            acc[c, i, first:last, :, here] = piece
                        else:
                            side_out[c, n - 1, i, first - lo : last - lo, :, here] = piece.astype(BF)
            else:
                both = jnp.concatenate([dk.reshape(16, 8, 128), dv.reshape(16, 8, 128)], axis=1)
                z_out[c, t - 5, :, :, here] = both.astype(BF)

        def query_grads():
            grad_q = lax.dot_general(all_tokens(0), dscores[half], TN, preferred_element_type=F32)
            grad_q = own_heads(grad_q) * 0.125
            gq_ref[:, :, there] = grad_q.T.astype(BF).reshape(8, 16, 128)

        passes = [score, exponential, weigh, back]
        steps = [[lambda t=t, f=f: f(t) for t in range(STEPS)] for f in passes]
        steps[2].append(attended)
        steps[3].append(query_grads)
        return steps

    def run(*lists):
        for n in range(max(len(steps) for steps in lists)):
            for steps in lists:
                if n < len(steps):
                    steps[n]()

    def attend_one(c, half):
        for steps in attend(c, half):
            run(steps)

    def attend_both(c):
        one, two = attend(c, 0), attend(c, 1)
        run(one[0])
        run(one[1], two[0])
        run(one[2], two[1])
        run(one[3], two[2])
        run(two[3])

    def load(c):
        gather_c(c, 1 - core).wait_recv()
        for first in range(2):
            block = gath[c, first].reshape(16, 16, LANES).astype(F32)
            for i in range(2):
                rows = block[:, i * 8 : i * 8 + 8].reshape(128, LANES).astype(BF)
                kv[c, i, ZONAL + first * 8 : ZONAL + first * 8 + 8] = rows.reshape(8, 16, LANES)
        for copy in edge_copies(c) + corner_copies(c):
            copy.wait_recv()

    def stage1(c):
        zonal_core(c).start()
        for copy in side_copies(c):
            copy.start()

    def stage2_zonal(c):
        zonal_core(c).wait_recv()
        z_mid1[c] = (z_out[c, core].astype(F32) + z_in1[c].astype(F32)).astype(BF)
        zonal_y(c).start()

    def stage2_side(c):
        for copy in side_copies(c):
            copy.wait_recv()
        for i in range(2):
            from_east = side_in[c, 0, i].astype(F32).reshape(REGION, 8, LANES)
            from_west = side_in[c, 1, i].astype(F32).reshape(REGION, 8, LANES)
            total = acc[c, i] + jnp.concatenate([from_west, from_east], axis=1)
            acc[c, i, 6:14] = total[6:14]
            lat_out[c, 0, i] = total[0:6].astype(BF)
            lat_out[c, 1, i] = total[14:20].astype(BF)
        to_up, to_down = grad_lat_copies(c)
        far_to_up, far_to_down = cross_grads(c)
        near = c == CHUNKS - 1

        @pl.when((lat > 0) & ((lat != middle) | near))
        def _():
            to_up.start()

        @pl.when(far_up & jnp.logical_not(near))
        def _():
            far_to_up.start()

        @pl.when((lat < lats - 1) & ((lat != middle - 1) | near))
        def _():
            to_down.start()

        @pl.when(far_down & jnp.logical_not(near))
        def _():
            far_to_down.start()

    def relay_grads(c):
        @pl.when(crosses)
        def _():
            cross_grads(c)[0].wait_recv()
            pass_on_grads(c).start()

    def stage3(c):
        zonal_y(c).wait_recv()
        z_mid2[c] = (z_mid1[c, pl.ds(why * ZN, ZN)].astype(F32) + z_in2[c].astype(F32)).astype(BF)
        for d in (4, 3, 5, 2, 6, 1, 7):
            zonal_z(c, d).start()

    def stage4(c):
        total = z_mid2[c, zed].astype(F32)
        for d in (1, 7, 2, 6, 3, 5, 4):
            zonal_z(c, d).wait_recv()
            total = total + z_in3[c, d].astype(F32)
        total = total * (COLS ** -0.5)
        to_up, to_down = grad_lat_copies(c)
        near = c == CHUNKS - 1

        @pl.when((lat < lats - 1) & ((lat != middle - 1) | near))
        def _():
            to_up.wait_recv()

        @pl.when((lat > 0) & ((lat != middle) | near))
        def _():
            to_down.wait_recv()

        @pl.when(crosses & jnp.logical_not(near))
        def _():
            pass_on_grads(c).wait_recv()

        for i, ref in enumerate((gk_ref, gv_ref)):
            for r in range(ROWS):
                row = acc[c, i, 6 + r] + total[i * 8 + r : i * 8 + r + 1, :]
                if r >= 2:
                    row = row + lat_in[c, 0, i, r - 2].astype(F32)
                if r < 6:
                    row = row + lat_in[c, 1, i, r].astype(F32)
                ref[r, :, lanes(c)] = row.astype(BF)

    @pl.loop(0, CHUNKS)
    def _(c):
        load(c)

        @pl.when(c == 0)
        def _():
            relay_rows(3)

        @pl.when(c < CHUNKS - 1)
        def _():
            prepare_b(c + 1)

        @pl.when(c < CHUNKS - 2)
        def _():
            send_pooled(c + 2)

        attend_both(c)
        stage1(c)

        @pl.when(c < CHUNKS - 2)
        def _():
            prepare_a(c + 2)

        @pl.when(c > 0)
        def _():
            stage2_zonal(c - 1)

        @pl.when(c > 1)
        def _():
            stage3(c - 2)

        @pl.when((c > 0) & (c < CHUNKS - 1))
        def _():
            stage2_side(c - 1)

    stage2_zonal(CHUNKS - 1)
    for store in stores:
        store.start()
    stage2_side(CHUNKS - 2)
    relay_grads(0)
    relay_grads(1)
    stage3(CHUNKS - 2)
    stage3(CHUNKS - 1)
    stage2_side(CHUNKS - 1)
    stage4(0)
    relay_grads(2)
    stage4(1)
    stage4(2)
    stage4(3)

    for store in stores:
        store.wait()

    @pl.loop(0, CHUNKS)
    def _(c):
        below, above = lat_copies(c)
        to_up, to_down = grad_lat_copies(c)

        @pl.when(lat < lats - 1)
        def _():
            for copy in below + [to_down]:
                copy.wait_send()

        @pl.when(lat > 0)
        def _():
            for copy in above + [to_up]:
                copy.wait_send()

        for copy in edge_copies(c) + corner_copies(c) + side_copies(c) + [zonal_core(c), zonal_y(c), gather_c(c, core)]:
            copy.wait_send()
        for d in range(1, ZN):
            zonal_z(c, d).wait_send()
            gather_z(c, d).wait_send()

        @pl.when(crosses & (c > 0))
        def _():
            pass_on(c).wait_send()

        @pl.when(crosses & (c < CHUNKS - 1))
        def _():
            pass_on_grads(c).wait_send()

    gather_y(why).wait_send()


def hand_over(*refs):
    for src, dst in zip(refs[:4], refs[4:]):
        dst[...] = src[...]


def body(queries, keys, values, cotangent, near_pattern, zonal_pattern):
    block = jax.ShapeDtypeStruct(queries.shape, BF)
    dma = pltpu.SemaphoreType.DMA
    vm = pltpu.VMEM
    scratch = [vm(queries.shape, BF)] * 6 + [dma((4,)), dma((2,))] + [
        vm((CHUNKS, 2, TILES, 16, LANES), BF),
        vm((CHUNKS, 2, 2, 4, 16, LANES), BF),
        vm((CHUNKS, 2, 2, 2, 3, 16, LANES), BF),
        vm((CHUNKS, 2, 2, ZN, 16, LANES), BF),
        vm((8, 640, 256), F32),
        vm((SECT * 8, 128), F32),
        vm((32, 512), F32),
        vm((16, SPAN, SPAN), jnp.int32),
        vm((2, TILES * 16, 256), F32),
        vm((2, TILES * 16, 256), BF),
        vm((2, TILES * 16, 256), BF),
        vm((CHUNKS, 2, REGION, 16, LANES), F32),
        vm((CHUNKS, 2, 2, 10, 16, LANES), BF),
        vm((CHUNKS, 2, 2, 10, 16, LANES), BF),
        vm((CHUNKS, 2, 2, 6, 16, LANES), BF),
        vm((CHUNKS, 2, 2, 6, 16, LANES), BF),
        vm((CHUNKS, 2, 16, 16, LANES), BF),
        vm((CHUNKS, 16, 16, LANES), BF),
        vm((CHUNKS, 16, 16, LANES), BF),
        vm((CHUNKS, 8, 16, LANES), BF),
        vm((CHUNKS, 8, 16, LANES), BF),
        vm((CHUNKS, 8, 16, LANES), BF),
        vm((CHUNKS, 2, 6, 16, LANES), BF),
        vm((CHUNKS, 2, 6, 16, LANES), BF),
    ]
    sems = [(CHUNKS, 2), (CHUNKS,), (CHUNKS,), (CHUNKS,), (CHUNKS, 4), (CHUNKS, 2), (CHUNKS, 4), (CHUNKS, ZN), (1,), (CHUNKS,), (CHUNKS, 2), (CHUNKS, 2), (CHUNKS,), (CHUNKS,), (CHUNKS, ZN)]
    for shape in sems:
        scratch += [dma(shape), dma(shape)]
    results = pl.pallas_call(
        kernel,
        out_shape=[block] * 4,
        in_specs=[pl.BlockSpec(memory_space=pl.ANY)] * 4 + [pl.BlockSpec(memory_space=pltpu.VMEM)] * 2,
        out_specs=[pl.BlockSpec(memory_space=pl.ANY)] * 2 + [pl.BlockSpec(memory_space=pltpu.VMEM)] * 2,
        scratch_shapes=scratch,
        compiler_params=pltpu.CompilerParams(
            collective_id=0, has_side_effects=True, vmem_limit_bytes=56 * 1024 * 1024
        ),
        cost_estimate=pl.CostEstimate(flops=3_000_000_000, bytes_accessed=2 << 20, transcendentals=1 << 20),
    )(queries, keys, values, cotangent, jnp.swapaxes(near_pattern, 0, 1), zonal_pattern)

    return pl.pallas_call(
        hand_over,
        out_shape=[block] * 4,
        in_specs=[pl.BlockSpec(memory_space=pltpu.VMEM)] * 4,
        out_specs=[pl.BlockSpec(memory_space=pltpu.VMEM)] * 4,
    )(*results)


def solution(mesh):
    grid = P("lat", "lon", None)
    return jax.shard_map(
        body,
        mesh=mesh,
        in_specs=(grid, grid, grid, grid, P(), P("lat", None)),
        out_specs=(grid, grid, grid, grid),
        check_vma=False,
    )
```
